512 devices in a mesh: grp: 16 (over y, core), pair: 32 (over x, z).
Axes of the slice: x: 4, y: 8, z: 8, core: 2. Of those that a mesh axis runs over, the one named last changes fastest.
Arguments:
- amplitudes: bfloat16 [2048, 10368], P('pair'), may hold values from -6 to 6
- integrals: bfloat16 [10368, 10368], P('pair', 'grp'), may hold values from -0.0625 to 0.0625
- hole_ints: bfloat16 [2048, 2048], replicated, may hold values from -0.125 to 0.125
- driver: bfloat16 [2048, 10368], P('pair', 'grp'), may hold values from -6 to 6
- e_occ: float32 [128], replicated, may hold values from -1.2 to -0.2
- e_virt: float32 [288], replicated, may hold values from 0.3 to 1.5
- occ_pairs: int32 [2, 2048], P(None, 'pair'), may hold values from 0 to 127
- virt_pairs: int32 [2, 10368], P(None, 'grp'), may hold values from 0 to 287
Outputs:
- amp_next: float32 [2048, 10368], P('pair')
The draws below stay inside these ranges and needn't reach their ends.
All inputs are finite; a program needn't handle non-finite values.
Results may differ from the reference program's by a relative error of at most 0.0003.
Values may be sent and summed in bfloat16 or wider, within the bound.
A program may use at most 128 MiB of HBM per device.

```python
import jax
import jax.numpy as jnp

OCC = 128
NV = 288
VP = 10368
PAIRS = 2048


def with_ends(drawn, stream_key, least, largest):
    longest = drawn.shape.index(max(drawn.shape))
    spots = []
    for shift in (0, 1):
        where = [jax.random.randint(jax.random.fold_in(stream_key, axis), (), 0, length) for axis, length in enumerate(drawn.shape)]
        where[longest] = (where[longest] + shift) % drawn.shape[longest]
        spots.append(tuple(where))
    return drawn.at[spots[0]].set(least).at[spots[1]].set(largest)


def levels(stream_key, dims, shards, smallest, high):
    loudness = 1.0
    for axis_at, parts in shards:
        steps = jax.random.uniform(jax.random.fold_in(jax.random.fold_in(stream_key, 6), axis_at), (parts,), jnp.float32, smallest / len(shards), high / len(shards))
        loudness = loudness * jnp.repeat(jnp.exp(steps), dims[axis_at] // parts).reshape((-1,) + (1,) * (len(dims) - 1 - axis_at))
    return loudness


def noise(stream_key, extent, scale, most, shards=(), kind=jnp.bfloat16):
    array = scale * jax.random.normal(stream_key, extent, jnp.float32)
    if shards:
        array = array * levels(stream_key, extent, shards, -0.22, 0.18)
    return jnp.clip(array, -most, most).astype(kind)


def setup_inputs(seed: int = 0) -> dict:
    key_of = jax.random.split(jax.random.key(seed), 9)
    return {
        "amplitudes": noise(key_of[0], (PAIRS, VP), 1.0, 6.0, ((0, 32),)),
        "integrals": noise(key_of[1], (VP, VP), VP ** -0.5, 0.0625, ((0, 32), (1, 16))),
        "hole_ints": noise(key_of[2], (PAIRS, PAIRS), PAIRS ** -0.5, 0.125),
        "driver": noise(key_of[3], (PAIRS, VP), 1.0, 6.0, ((0, 32), (1, 16))),
        "e_occ": jnp.clip(jax.random.uniform(key_of[4], (OCC,), jnp.float32, -1.2, -0.2), -1.2, -0.2),
        "e_virt": jnp.clip(jax.random.uniform(key_of[5], (NV,), jnp.float32, 0.3, 1.5), 0.3, 1.5),
        "occ_pairs": with_ends(jax.random.randint(key_of[6], (2, PAIRS), 0, OCC), jax.random.fold_in(key_of[6], 1), 0, OCC - 1).astype(jnp.int32),
        "virt_pairs": with_ends(jax.random.randint(key_of[7], (2, VP), 0, NV), jax.random.fold_in(key_of[7], 1), 0, NV - 1).astype(jnp.int32),
    }


def reference(amplitudes, integrals, hole_ints, driver, e_occ, e_virt, occ_pairs, virt_pairs):
    particle = jnp.dot(amplitudes, integrals, preferred_element_type=jnp.float32)
    hole_term = jnp.dot(hole_ints, amplitudes, preferred_element_type=jnp.float32)
    ladder = particle + hole_term
    hole_energy = e_occ[occ_pairs[0]] + e_occ[occ_pairs[1]]
    pair_energy = e_virt[virt_pairs[0]] + e_virt[virt_pairs[1]]
    energy_gap = pair_energy[None, :] - hole_energy[:, None]
    return (driver.astype(jnp.float32) + ladder) / energy_gap
```

```python
import functools

import jax
import jax.numpy as jnp
from jax import lax
from jax.experimental import pallas as pl
from jax.experimental.pallas import tpu as pltpu
from jax.sharding import PartitionSpec as P

MESH = pl.DeviceIdType.MESH
NX, NY, NZ = 4, 8, 8
ROWS = 64
DEPTH = 324
COLS = 648
LANES = 384
FRAME = 768
TALL = 656
VP = 10368
CHUNKS = ((0, 256, 256, 256), (256, 256, 256, 256), (512, 136, 144, 256))
FAR = (4, 3, 5, 2, 6, 1, 7)


def ladder_kernel(
    amp, ints, holes, drv, eocc, evirt, opairs, vpairs, out,
    amp_in, ints_in, drv_in, hole_win, eocc_in, evirt_in, opairs_in, vpairs_in,
    vt, ra, ap, al, part, rs, fin, fr, gap,
    in_sem, x_send, x_recv, a_send, a_recv, ad_send, ad_recv,
    z_send, z_recv, y_send, y_recv, c_send, c_recv, o_sem,
):
    grp, pair = lax.axis_index("grp"), lax.axis_index("pair")
    y, core = grp // 2, lax.rem(grp, 2)
    x, z = pair // NZ, lax.rem(pair, NZ)

    def at_x(d):
        return (grp, lax.rem(x + d, NX) * NZ + z)

    def at_z(d):
        return (grp, x * NZ + lax.rem(z + d, NZ))

    def at_y(d):
        return (lax.rem(y + d, NY) * 2 + core, pair)

    sibling = (y * 2 + 1 - core, pair)

    barrier = pltpu.get_barrier_semaphore()
    peers = [at_x(d) for d in (1, 2, 3)] + [at_z(d) for d in FAR]
    peers += [at_y(d) for d in FAR] + [sibling]
    for peer in peers:
        pl.semaphore_signal(barrier, inc=1, device_id=peer, device_id_type=MESH)

    loads = [
        pltpu.make_async_copy(ints, ints_in, in_sem.at[0]),
        pltpu.make_async_copy(amp, amp_in, in_sem.at[1]),
        pltpu.make_async_copy(drv, drv_in, in_sem.at[2]),
        pltpu.make_async_copy(eocc, eocc_in, in_sem.at[3]),
        pltpu.make_async_copy(evirt, evirt_in, in_sem.at[4]),
        pltpu.make_async_copy(opairs, opairs_in, in_sem.at[5]),
        pltpu.make_async_copy(vpairs, vpairs_in, in_sem.at[6]),
    ]
    for k in range(NX):
        rows = pl.ds(pl.multiple_of(x * NZ * ROWS, NZ * ROWS), NZ * ROWS)
        cols = pl.ds(pl.multiple_of((k * NZ + z) // 2 * 128, 128), 128)
        loads.append(
            pltpu.make_async_copy(holes.at[rows, cols], hole_win.at[k], in_sem.at[7 + k])
        )
    for load in loads:
        load.start()

    half = pl.multiple_of(lax.rem(z, 2) * ROWS, ROWS)
    other = pl.multiple_of(ROWS - lax.rem(z, 2) * ROWS, ROWS)

    loads[0].wait()
    vt[x] = jnp.zeros((TALL, LANES), jnp.bfloat16)
    vt[x, 0:COLS, 0:DEPTH] = ints_in[...]

    loads[1].wait()
    start = pl.multiple_of(grp * (COLS // 128) * 128, 128)
    window = amp_in[:, pl.ds(start, FRAME)].astype(jnp.float32)
    window = pltpu.roll(window, lax.rem(FRAME - grp * (COLS % 128), FRAME), axis=1)
    for k in range(NX):
        ra[k, pl.ds(other, ROWS), :] = jnp.zeros((ROWS, FRAME), jnp.bfloat16)
    ra[x, pl.ds(half, ROWS), :] = window.astype(jnp.bfloat16)

    ap[...] = jnp.zeros(ap.shape, jnp.bfloat16)
    for k in range(NX):
        for t in range(NZ):
            first = (k * NZ + t) * DEPTH
            ap[t, k, :, 0:DEPTH] = amp_in[:, first : first + DEPTH]

    pl.semaphore_wait(barrier, len(peers))

    started = []

    def send(src, dst, send_sem, recv_sem, device):
        copy = pltpu.make_async_remote_copy(
            src_ref=src, dst_ref=dst, send_sem=send_sem, recv_sem=recv_sem,
            device_id=device, device_id_type=MESH,
        )
        copy.start()
        started.append(copy)
        return copy

    both = pl.ds(2 * core, 2)
    a_copies = [
        send(ap.at[lax.rem(z + d, NZ), both], al.at[z, both],
             a_send.at[d - 1], a_recv.at[d - 1], at_z(d))
        for d in FAR
    ]
    x_copies = []
    for c, (first, _, tall, wide) in enumerate(CHUNKS):
        copies = []
        for d in (2, 1, 3):
            rows = (x, pl.ds(first, tall))
            copies.append(send(vt.at[rows], vt.at[rows], x_send.at[c, d - 1, 0],
                               x_recv.at[c, d - 1, 0], at_x(d)))
            cells = (x, pl.ds(half, ROWS), pl.ds(first, wide))
            copies.append(send(ra.at[cells], ra.at[cells], x_send.at[c, d - 1, 1],
                               x_recv.at[c, d - 1, 1], at_x(d)))
        x_copies.append(copies)

    al[z] = ap[z]

    for load in loads[2:]:
        load.wait()
    orbital = lax.broadcasted_iota(jnp.int32, (128, 128), 0)
    diagonal = orbital == lax.broadcasted_iota(jnp.int32, (128, 128), 1)

    def column(row):
        spread = jnp.where(diagonal, jnp.broadcast_to(row, (128, 128)), 0.0)
        return jnp.sum(spread, axis=1, keepdims=True)

    occ = column(eocc_in[...])
    hole_row = jnp.zeros((1, ROWS), jnp.float32)
    for s in range(2):
        labels = jnp.broadcast_to(opairs_in[s : s + 1, :], (128, ROWS))
        table = lax.broadcasted_iota(jnp.int32, (128, ROWS), 0)
        picked = jnp.where(labels == table, jnp.broadcast_to(occ, (128, ROWS)), 0.0)
        hole_row = hole_row + jnp.sum(picked, axis=0, keepdims=True)
    square = lax.broadcasted_iota(jnp.int32, (ROWS, ROWS), 0)
    square = square == lax.broadcasted_iota(jnp.int32, (ROWS, ROWS), 1)
    hole_col = jnp.sum(
        jnp.where(square, jnp.broadcast_to(hole_row, (ROWS, ROWS)), 0.0),
        axis=1, keepdims=True,
    )
    pair_row = jnp.zeros((1, COLS), jnp.float32)
    for s in range(2):
        labels = jnp.broadcast_to(vpairs_in[s : s + 1, :], (128, COLS))
        table = lax.broadcasted_iota(jnp.int32, (128, COLS), 0)
        picked = jnp.zeros((128, COLS), jnp.float32)
        for b in range(3):
            virt = jnp.broadcast_to(column(evirt_in[:, 128 * b : 128 * b + 128]), (128, COLS))
            picked = jnp.where(labels == table + 128 * b, virt, picked)
        pair_row = pair_row + jnp.sum(picked, axis=0, keepdims=True)
    gap[...] = pair_row - hole_col

    ad_copies = []
    for copy, d in zip(a_copies, FAR):
        copy.wait_recv()
        slot = al.at[lax.rem(z + NZ - d, NZ), both]
        ad_copies.append(send(slot, slot, ad_send.at[d - 1], ad_recv.at[d - 1], sibling))
    for copy in ad_copies:
        copy.wait_recv()

    z_copies = [None] * len(CHUNKS)
    y_copies = [None] * len(CHUNKS)

    def multiply(c):
        first, _, tall, wide = CHUNKS[c]
        for copy in x_copies[c]:
            copy.wait_recv()
        total = jnp.zeros((NZ * ROWS, tall), jnp.float32)
        for k in range(NX):
            total = total + lax.dot_general(
                al[:, k].reshape(NZ * ROWS, LANES), vt[k, first : first + tall, :],
                (((1,), (1,)), ((), ())), preferred_element_type=jnp.float32,
            )
            total = total + jnp.dot(
                hole_win[k], ra[k, :, first : first + tall],
                preferred_element_type=jnp.float32,
            )
        part[c, :, :, 0:tall] = total.reshape(NZ, ROWS, tall)
        z_copies[c] = [
            send(part.at[c, lax.rem(z + d, NZ)], rs.at[c, d - 1],
                 z_send.at[c, d - 1], z_recv.at[c, d - 1], at_z(d))
            for d in FAR
        ]

    def update(c):
        first, count, _, wide = CHUNKS[c]
        total = part[c, z, :, 0:count]
        for copy, d in zip(z_copies[c], FAR):
            copy.wait_recv()
            total = total + rs[c, d - 1, :, 0:count]
        driver = drv_in[:, first : first + count].astype(jnp.float32)
        fin[c, :, 0:count] = (driver + total) / gap[:, first : first + count]
        cols = pl.ds(first, wide)
        y_copies[c] = [
            send(fin.at[c], fr.at[d, :, cols], y_send.at[c, d - 1], y_recv.at[c, d - 1], at_y(d))
            for d in FAR
        ]
        c_copies.append(send(fin.at[c], out.at[grp, :, cols],
                             c_send.at[c, 0], c_recv.at[c, 0], sibling))
        copy = pltpu.make_async_copy(fin.at[c], out.at[grp, :, cols], o_sem.at[c, 0])
        copy.start()
        o_copies.append(copy)

    c_copies, o_copies = [], []

    def spread(c):
        first, _, _, wide = CHUNKS[c]
        cols = pl.ds(first, wide)
        for copy, d in zip(y_copies[c], FAR):
            copy.wait_recv()
            owner = lax.rem(y + NY - d, NY) * 2 + core
            c_copies.append(send(fr.at[d, :, cols], out.at[owner, :, cols],
                                 c_send.at[c, d], c_recv.at[c, d], sibling))
            copy = pltpu.make_async_copy(fr.at[d, :, cols], out.at[owner, :, cols], o_sem.at[c, d])
            copy.start()
            o_copies.append(copy)

    multiply(0)
    multiply(1)
    update(0)
    multiply(2)
    update(1)
    update(2)
    for c in range(len(CHUNKS)):
        spread(c)
    for copy in c_copies:
        copy.wait_recv()
    for copy in o_copies:
        copy.wait()
    for copy in started:
        copy.wait_send()


def place_kernel(blocks, out):
    for g in range(2 * NY):
        out[:, COLS * g : COLS * (g + 1)] = blocks[g, :, 0:COLS]


def shards(amplitudes, integrals, hole_ints, driver, e_occ, e_virt, occ_pairs, virt_pairs):
    chunks = len(CHUNKS)
    dma = pltpu.SemaphoreType.DMA
    virt = jnp.pad(e_virt, (0, 96)).reshape(1, 384)
    blocks = pl.pallas_call(
        ladder_kernel,
        out_shape=jax.ShapeDtypeStruct((2 * NY, ROWS, FRAME), jnp.float32),
        in_specs=[pl.BlockSpec(memory_space=pl.ANY)] * 8,
        out_specs=pl.BlockSpec(memory_space=pl.ANY),
        scratch_shapes=[
            pltpu.VMEM((ROWS, VP), jnp.bfloat16),
            pltpu.VMEM((COLS, DEPTH), jnp.bfloat16),
            pltpu.VMEM((ROWS, COLS), jnp.bfloat16),
            pltpu.VMEM((NX, NZ * ROWS, 128), jnp.bfloat16),
            pltpu.VMEM((1, 128), jnp.float32),
            pltpu.VMEM((1, 384), jnp.float32),
            pltpu.VMEM((2, ROWS), jnp.int32),
            pltpu.VMEM((2, COLS), jnp.int32),
            pltpu.VMEM((NX, TALL, LANES), jnp.bfloat16),
            pltpu.VMEM((NX, 2 * ROWS, FRAME), jnp.bfloat16),
            pltpu.VMEM((NZ, NX, ROWS, LANES), jnp.bfloat16),
            pltpu.VMEM((NZ, NX, ROWS, LANES), jnp.bfloat16),
            pltpu.VMEM((chunks, NZ, ROWS, 256), jnp.float32),
            pltpu.VMEM((chunks, NZ - 1, ROWS, 256), jnp.float32),
            pltpu.VMEM((chunks, ROWS, 256), jnp.float32),
            pltpu.VMEM((NY, ROWS, FRAME), jnp.float32),
            pltpu.VMEM((ROWS, COLS), jnp.float32),
            dma((11,)),
            dma((chunks, 3, 2)), dma((chunks, 3, 2)),
            dma((7,)), dma((7,)),
            dma((7,)), dma((7,)),
            dma((chunks, 7)), dma((chunks, 7)),
            dma((chunks, 7)), dma((chunks, 7)),
            dma((chunks, 8)), dma((chunks, 8)),
            dma((chunks, 8)),
        ],
        compiler_params=pltpu.CompilerParams(
            collective_id=0, has_side_effects=True, vmem_limit_bytes=40 * 2**20
        ),
        cost_estimate=pl.CostEstimate(
            flops=2 * NZ * ROWS * 4 * (DEPTH + ROWS) * COLS,
            bytes_accessed=8 * 2**20, transcendentals=0,
        ),
    )(
        amplitudes, integrals.T, hole_ints, driver, e_occ.reshape(1, 128), virt,
        occ_pairs, virt_pairs,
    )
    tall = 16
    return pl.pallas_call(
        place_kernel,
        grid=(ROWS // tall,),
        out_shape=jax.ShapeDtypeStruct((ROWS, VP), jnp.float32),
        in_specs=[pl.BlockSpec((2 * NY, tall, FRAME), lambda i: (0, i, 0))],
        out_specs=pl.BlockSpec((tall, VP), lambda i: (i, 0)),
        compiler_params=pltpu.CompilerParams(vmem_limit_bytes=32 * 2**20),
    )(blocks)


def solution(mesh):
    placed = (
        P("pair", None),
        P("pair", "grp"),
        P(),
        P("pair", "grp"),
        P(),
        P(),
        P(None, "pair"),
        P(None, "grp"),
    )
    return jax.shard_map(
        shards, mesh=mesh, in_specs=placed, out_specs=P("pair", None), check_vma=False
    )
```

```python
import jax
import jax.numpy as jnp
from jax import lax
from jax.experimental import pallas as pl
from jax.experimental.pallas import tpu as pltpu
from jax.sharding import PartitionSpec as P

MESH = pl.DeviceIdType.MESH
NX, NY, NZ = 4, 8, 8
ROWS = 64
SET = NZ * ROWS
DEPTH = 324
COLS = 648
LANES = 384
FRAME = 768
TALL = 656
VP = 10368
WIDE = 256
LAST = 2 * WIDE
REST = COLS - LAST - 128
PACKED = ROWS + REST
FAR = (4, 3, 5, 2, 6, 1, 7)


def ladder_kernel(
    amp, ints, holes, drv, eocc, evirt, opairs, vpairs, out, out_last,
    amp_in, ints_in, drv_in, hole_win, eocc_in, evirt_in, opairs_in, vpairs_in,
    vt, ra, ap, al, part, part_last, via3, via4, rs, rs_last,
    fin, fin_last, fr, fr_last, gap, gap_last, drv_last,
    in_sem, x_send, x_recv, a_send, a_recv, ay_send, ay_recv, ad_send, ad_recv,
    z_send, z_recv, zl_send, zl_recv, y_send, y_recv, yl_send, yl_recv,
    c_send, c_recv, cl_send, cl_recv, o_sem, ol_sem,
):
    grp, pair = lax.axis_index("grp"), lax.axis_index("pair")
    y, core = grp // 2, lax.rem(grp, 2)
    x, z = pair // NZ, lax.rem(pair, NZ)

    def at_x(d):
        return (grp, lax.rem(x + d, NX) * NZ + z)

    def at_z(d):
        return (grp, x * NZ + lax.rem(z + d, NZ))

    def at_y(d):
        return (lax.rem(y + d, NY) * 2 + core, pair)

    sibling = (y * 2 + 1 - core, pair)

    barrier = pltpu.get_barrier_semaphore()
    peers = [at_x(d) for d in (1, 2, 3)] + [at_z(d) for d in FAR]
    peers += [at_y(d) for d in FAR] + [sibling]
    for peer in peers:
        pl.semaphore_signal(barrier, inc=1, device_id=peer, device_id_type=MESH)

    loads = [
        pltpu.make_async_copy(ints, ints_in, in_sem.at[0]),
        pltpu.make_async_copy(amp, amp_in, in_sem.at[1]),
        pltpu.make_async_copy(drv, drv_in, in_sem.at[2]),
        pltpu.make_async_copy(eocc, eocc_in, in_sem.at[3]),
        pltpu.make_async_copy(evirt, evirt_in, in_sem.at[4]),
        pltpu.make_async_copy(opairs, opairs_in, in_sem.at[5]),
        pltpu.make_async_copy(vpairs, vpairs_in, in_sem.at[6]),
    ]
    for k in range(NX):
        rows = pl.ds(pl.multiple_of(x * SET, SET), SET)
        cols = pl.ds(pl.multiple_of((k * NZ + z) // 2 * 128, 128), 128)
        loads.append(
            pltpu.make_async_copy(holes.at[rows, cols], hole_win.at[k], in_sem.at[7 + k])
        )
    for load in loads:
        load.start()

    half = pl.multiple_of(lax.rem(z, 2) * ROWS, ROWS)
    other = pl.multiple_of(ROWS - lax.rem(z, 2) * ROWS, ROWS)
    started = []

    def send(src, dst, send_sem, recv_sem, device):
        copy = pltpu.make_async_remote_copy(
            src_ref=src, dst_ref=dst, send_sem=send_sem, recv_sem=recv_sem,
            device_id=device, device_id_type=MESH,
        )
        copy.start()
        started.append(copy)
        return copy

    loads[0].wait()
    vt[x, COLS:TALL, :] = jnp.zeros((TALL - COLS, LANES), jnp.bfloat16)
    vt[x, 0:COLS, 256:LANES] = jnp.zeros((COLS, LANES - 256), jnp.bfloat16)
    vt[x, 0:COLS, 0:DEPTH] = ints_in[...]

    loads[1].wait()
    start = pl.multiple_of(grp * (COLS // 128) * 128, 128)
    window = amp_in[:, pl.ds(start, FRAME)].astype(jnp.float32)
    window = pltpu.roll(window, lax.rem(FRAME - grp * (COLS % 128), FRAME), axis=1)
    for k in range(NX):
        ra[k, pl.ds(other, ROWS), :] = jnp.zeros((ROWS, FRAME), jnp.bfloat16)
    ra[x, pl.ds(half, ROWS), :] = window.astype(jnp.bfloat16)

    for k in range(NX):
        for t in range(NZ):
            first = (k * NZ + t) * DEPTH
            ap[t, k, :, 256:LANES] = jnp.zeros((ROWS, LANES - 256), jnp.bfloat16)
            ap[t, k, :, 0:DEPTH] = amp_in[:, first : first + DEPTH]

    pl.semaphore_wait(barrier, len(peers))

    both = pl.ds(2 * core, 2)
    unit = y // 2
    unit_rows = pl.ds(pl.multiple_of(lax.rem(y, 2) * 32 + core * 16, 16), 16)
    far_copies = [
        send(ap.at[lax.rem(z + d, NZ), unit, unit_rows], al.at[NZ - d, unit, unit_rows],
             a_send.at[d - 1], a_recv.at[d - 1], at_z(d))
        for d in (4, 3, 5)
    ]

    def x_parts(c, which, part_of=None):
        first, tall, wide = c * WIDE, WIDE, WIDE
        if c == 2:
            tall = TALL - LAST
        if part_of is not None:
            first, tall, wide = first + 128 * part_of, 128, 128
        return vt.at[which, pl.ds(first, tall)], ra.at[which, pl.ds(half, ROWS), pl.ds(first, wide)]

    def x_sends(c, which, d, slot, part_of=None):
        return [
            send(ref, ref, x_send.at[c, slot, i], x_recv.at[c, slot, i], at_x(d))
            for i, ref in enumerate(x_parts(c, which, part_of))
        ]

    x_copies = [[], [], []]

    def x_first(c):
        x_copies[c] = [x_sends(c, x, 1, 0), x_sends(c, x, 3, 1)]

    def x_second(c):
        for copies in x_copies[c]:
            for copy in copies:
                copy.wait_recv()
        x_copies[c] = [
            x_sends(c, lax.rem(x + 3, NX), 1, 2, 0),
            x_sends(c, lax.rem(x + 1, NX), 3, 3, 1),
        ]

    x_first(0)
    near_copies = [
        send(ap.at[lax.rem(z + d, NZ), both], al.at[NZ - d, both],
             a_send.at[d - 1], a_recv.at[d - 1], at_z(d))
        for d in (2, 6, 1, 7)
    ]
    x_first(1)
    x_copies[2] = [x_sends(2, x, d, d - 1) for d in (2, 1, 3)]

    al[0] = ap[z]

    for load in loads[2:]:
        load.wait()
    orbital = lax.broadcasted_iota(jnp.int32, (128, 128), 0)
    diagonal = orbital == lax.broadcasted_iota(jnp.int32, (128, 128), 1)

    def column(row):
        spread = jnp.where(diagonal, jnp.broadcast_to(row, (128, 128)), 0.0)
        return jnp.sum(spread, axis=1, keepdims=True)

    occ = column(eocc_in[...])
    hole_row = jnp.zeros((1, ROWS), jnp.float32)
    for s in range(2):
        labels = jnp.broadcast_to(opairs_in[s : s + 1, :], (128, ROWS))
        table = lax.broadcasted_iota(jnp.int32, (128, ROWS), 0)
        picked = jnp.where(labels == table, jnp.broadcast_to(occ, (128, ROWS)), 0.0)
        hole_row = hole_row + jnp.sum(picked, axis=0, keepdims=True)
    square = lax.broadcasted_iota(jnp.int32, (ROWS, ROWS), 0)
    square = square == lax.broadcasted_iota(jnp.int32, (ROWS, ROWS), 1)
    hole_col = jnp.sum(
        jnp.where(square, jnp.broadcast_to(hole_row, (ROWS, ROWS)), 0.0),
        axis=1, keepdims=True,
    )
    padded = jnp.concatenate([evirt_in[...], jnp.zeros((1, 96), jnp.float32)], axis=1)
    virts = [column(padded[:, 128 * b : 128 * b + 128]) for b in range(3)]
    pair_row = jnp.zeros((1, COLS), jnp.float32)
    for s in range(2):
        labels = jnp.broadcast_to(vpairs_in[s : s + 1, :], (128, COLS))
        table = lax.broadcasted_iota(jnp.int32, (128, COLS), 0)
        picked = jnp.zeros((128, COLS), jnp.float32)
        for b in range(3):
            virt = jnp.broadcast_to(virts[b], (128, COLS))
            picked = jnp.where(labels == table + 128 * b, virt, picked)
        pair_row = pair_row + jnp.sum(picked, axis=0, keepdims=True)
    gap[...] = pair_row - hole_col

    def turned(block):
        tile = jnp.concatenate([block, jnp.zeros((ROWS, 128 - REST), jnp.float32)], axis=1)
        tile = jnp.concatenate([tile, jnp.zeros((128 - ROWS, 128), jnp.float32)], axis=0)
        return jnp.transpose(tile)[0:REST, 0:ROWS]

    gap_last[...] = jnp.ones(gap_last.shape, jnp.float32)
    gap_last[0:ROWS, :] = gap[:, LAST : LAST + 128]
    gap_last[ROWS:PACKED, 0:ROWS] = turned(gap[:, COLS - REST : COLS])
    drv_last[...] = jnp.zeros(drv_last.shape, jnp.float32)
    drv_last[0:ROWS, :] = drv_in[:, LAST : LAST + 128].astype(jnp.float32)
    drv_last[ROWS:PACKED, 0:ROWS] = turned(drv_in[:, COLS - REST : COLS].astype(jnp.float32))

    ad_copies = []

    def share(ref, slot):
        ad_copies.append(send(ref, ref, ad_send.at[slot], ad_recv.at[slot], sibling))

    far = pl.ds(3, 3)
    for copy in far_copies:
        copy.wait_recv()
    own = al.at[far, unit, unit_rows]
    ay_copies = [
        send(own, own, ay_send.at[d - 1], ay_recv.at[d - 1], at_y(d)) for d in FAR
    ]
    share(own, 0)
    x_second(0)
    for slot, (copy, d) in enumerate(zip(near_copies, (2, 6, 1, 7))):
        copy.wait_recv()
        share(al.at[NZ - d, both], 8 + slot)
    x_second(1)
    for copy, d in zip(ay_copies, FAR):
        copy.wait_recv()
        there = lax.rem(y + NY - d, NY)
        rows = pl.ds(pl.multiple_of(lax.rem(there, 2) * 32 + core * 16, 16), 16)
        share(al.at[far, there // 2, rows], d)
    for copy in ad_copies:
        copy.wait_recv()

    def product(c, first, tall, wide):
        for copies in x_copies[c]:
            for copy in copies:
                copy.wait_recv()
        total = jnp.zeros((SET, wide), jnp.float32)
        for k in range(NX):
            total = total + lax.dot_general(
                al[:, k].reshape(SET, LANES), vt[k, first : first + tall, :],
                (((1,), (1,)), ((), ())), preferred_element_type=jnp.float32,
            )
            lines = [
                hole_win[k, pl.ds(pl.multiple_of(lax.rem(z + r, NZ) * ROWS, ROWS), ROWS), :]
                for r in range(NZ)
            ]
            total = total + jnp.dot(
                jnp.concatenate(lines, axis=0), ra[k, :, first : first + wide],
                preferred_element_type=jnp.float32,
            )
        return total

    z_copies, y_copies = [None, None], [None, None]
    c_copies, o_copies = [], []

    def multiply(c):
        part[c] = product(c, c * WIDE, WIDE, WIDE).reshape(NZ, ROWS, WIDE)
        z_copies[c] = [
            send(part.at[c, 4, :, pl.ds(0, 128)], via4.at[c, 0], z_send.at[c, 0], z_recv.at[c, 0], at_z(2)),
            send(part.at[c, 4, :, pl.ds(128, 128)], via4.at[c, 1], z_send.at[c, 1], z_recv.at[c, 1], at_z(6)),
            send(part.at[c, 3], via3.at[c, 0], z_send.at[c, 2], z_recv.at[c, 2], at_z(1)),
            send(part.at[c, 5], via3.at[c, 1], z_send.at[c, 3], z_recv.at[c, 3], at_z(7)),
            send(part.at[c, 1], rs.at[c, 0], z_send.at[c, 4], z_recv.at[c, 4], at_z(1)),
            send(part.at[c, 7], rs.at[c, 1], z_send.at[c, 5], z_recv.at[c, 5], at_z(7)),
        ]

    def relay(c):
        for copy in z_copies[c][:4]:
            copy.wait_recv()
        part[c, 2] = part[c, 2] + via3[c, 0]
        part[c, 2, :, 0:128] = part[c, 2, :, 0:128] + via4[c, 0]
        part[c, 6] = part[c, 6] + via3[c, 1]
        part[c, 6, :, 128:256] = part[c, 6, :, 128:256] + via4[c, 1]
        z_copies[c] = z_copies[c][4:] + [
            send(part.at[c, 2], rs.at[c, 2], z_send.at[c, 6], z_recv.at[c, 6], at_z(2)),
            send(part.at[c, 6], rs.at[c, 3], z_send.at[c, 7], z_recv.at[c, 7], at_z(6)),
        ]

    def update(c):
        first = c * WIDE
        for copy in z_copies[c]:
            copy.wait_recv()
        total = part[c, 0] + ((rs[c, 0] + rs[c, 1]) + (rs[c, 2] + rs[c, 3]))
        driver = drv_in[:, first : first + WIDE].astype(jnp.float32)
        fin[c] = (driver + total) / gap[:, first : first + WIDE]
        cols = pl.ds(first, WIDE)
        y_copies[c] = [
            send(fin.at[c], fr.at[d, :, cols], y_send.at[c, i], y_recv.at[c, i], at_y(d))
            for i, d in enumerate((2, 6, 1, 7))
        ]
        keep(fin.at[c], 0, c)

    def y_relay(c):
        for copy in y_copies[c][:2]:
            copy.wait_recv()
        first = c * WIDE
        cols = pl.ds(first, WIDE)
        left, right = pl.ds(first, 128), pl.ds(first + 128, 128)
        moves = (
            (fr.at[2, :, left], fr.at[4, :, left], 2),
            (fr.at[6, :, right], fr.at[4, :, right], 6),
            (fr.at[2, :, cols], fr.at[3, :, cols], 1),
            (fr.at[6, :, cols], fr.at[5, :, cols], 7),
        )
        y_copies[c] += [
            send(src, dst, y_send.at[c, 4 + i], y_recv.at[c, 4 + i], at_y(d))
            for i, (src, dst, d) in enumerate(moves)
        ]

    def keep(ref, d, c):
        owner = lax.rem(y + NY - d, NY) * 2 + core
        dst = out.at[owner, :, pl.ds(c * WIDE, WIDE)] if c < 2 else out_last.at[owner]
        sems = (c_send.at[c, d], c_recv.at[c, d], o_sem.at[c, d])
        if c == 2:
            sems = (cl_send.at[d], cl_recv.at[d], ol_sem.at[d])
        c_copies.append(send(ref, dst, sems[0], sems[1], sibling))
        copy = pltpu.make_async_copy(ref, dst, sems[2])
        copy.start()
        o_copies.append(copy)

    def spread(c):
        cols = pl.ds(c * WIDE, WIDE)
        first, second = y_copies[c][:4], y_copies[c][4:]
        for copy, d in zip(first[2:], (1, 7)):
            copy.wait_recv()
            keep(fr.at[d, :, cols], d, c)
        for d in (2, 6):
            keep(fr.at[d, :, cols], d, c)
        for copy, d in zip(second[2:], (3, 5)):
            copy.wait_recv()
            keep(fr.at[d, :, cols], d, c)
        for copy in second[:2]:
            copy.wait_recv()
        keep(fr.at[4, :, cols], 4, c)

    def multiply_last():
        total = product(2, LAST, TALL - LAST, TALL - LAST)
        part_last[:, 0:ROWS, :] = total[:, 0:128].reshape(NZ, ROWS, 128)
        rest = jnp.concatenate(
            [total[:, 128:144], jnp.zeros((SET, 112), jnp.float32)], axis=1
        )
        for b in range(SET // 128):
            tile = jnp.transpose(rest[128 * b : 128 * b + 128])[0:REST]
            part_last[2 * b, ROWS:PACKED, 0:ROWS] = tile[:, 0:ROWS]
            part_last[2 * b + 1, ROWS:PACKED, 0:ROWS] = tile[:, ROWS : 2 * ROWS]
        return [
            send(part_last.at[d], rs_last.at[d - 1], zl_send.at[d - 1], zl_recv.at[d - 1], at_z(d))
            for d in FAR
        ]

    def update_last(copies):
        total = part_last[0]
        for copy, d in zip(copies, FAR):
            copy.wait_recv()
            total = total + rs_last[d - 1]
        fin_last[...] = (drv_last[...] + total) / gap_last[...]
        copies = [
            send(fin_last, fr_last.at[d], yl_send.at[d - 1], yl_recv.at[d - 1], at_y(d))
            for d in FAR
        ]
        keep(fin_last, 0, 2)
        return copies

    def spread_last(copies):
        for copy, d in zip(copies, FAR):
            copy.wait_recv()
            keep(fr_last.at[d], d, 2)

    part_last[:, ROWS:PACKED, :] = jnp.zeros((NZ, REST, 128), jnp.float32)
    multiply(0)
    multiply(1)
    relay(0)
    relay(1)
    update(0)
    last = multiply_last()
    update(1)
    y_relay(0)
    last = update_last(last)
    y_relay(1)
    spread(0)
    spread(1)
    spread_last(last)
    for copy in c_copies:
        copy.wait_recv()
    for copy in o_copies:
        copy.wait()
    for copy in started:
        copy.wait_send()


def place_kernel(blocks, last, out, rest):
    tall = out.shape[0]
    step = pl.program_id(0)

    @pl.when(step == 0)
    def _():
        for g in range(2 * NY):
            tile = jnp.concatenate(
                [last[g, ROWS:PACKED, :], jnp.zeros((128 - REST, 128), jnp.float32)], axis=0
            )
            rest[g] = jnp.transpose(tile)[0:ROWS, :]

    rows = pl.ds(pl.multiple_of(step * tall, tall), tall)
    for g in range(2 * NY):
        first = COLS * g
        out[:, first : first + LAST] = blocks[g]
        out[:, first + LAST : first + LAST + 128] = last[g, rows, :]
        out[:, first + COLS - REST : first + COLS] = rest[g, rows, 0:REST]


def shards(amplitudes, integrals, hole_ints, driver, e_occ, e_virt, occ_pairs, virt_pairs):
    dma = pltpu.SemaphoreType.DMA
    bf16, f32 = jnp.bfloat16, jnp.float32
    blocks, last = pl.pallas_call(
        ladder_kernel,
        out_shape=[
            jax.ShapeDtypeStruct((2 * NY, ROWS, LAST), f32),
            jax.ShapeDtypeStruct((2 * NY, PACKED, 128), f32),
        ],
        in_specs=[pl.BlockSpec(memory_space=pl.ANY)] * 8,
        out_specs=[pl.BlockSpec(memory_space=pl.ANY)] * 2,
        scratch_shapes=[
            pltpu.VMEM((ROWS, VP), bf16),
            pltpu.VMEM((COLS, DEPTH), bf16),
            pltpu.VMEM((ROWS, COLS), bf16),
            pltpu.VMEM((NX, SET, 128), bf16),
            pltpu.VMEM((1, 128), f32),
            pltpu.VMEM((1, 288), f32),
            pltpu.VMEM((2, ROWS), jnp.int32),
            pltpu.VMEM((2, COLS), jnp.int32),
            pltpu.VMEM((NX, TALL, LANES), bf16),
            pltpu.VMEM((NX, 2 * ROWS, FRAME), bf16),
            pltpu.VMEM((NZ, NX, ROWS, LANES), bf16),
            pltpu.VMEM((NZ, NX, ROWS, LANES), bf16),
            pltpu.VMEM((2, NZ, ROWS, WIDE), f32),
            pltpu.VMEM((NZ, PACKED, 128), f32),
            pltpu.VMEM((2, 2, ROWS, WIDE), f32),
            pltpu.VMEM((2, 2, ROWS, 128), f32),
            pltpu.VMEM((2, 4, ROWS, WIDE), f32),
            pltpu.VMEM((NZ - 1, PACKED, 128), f32),
            pltpu.VMEM((2, ROWS, WIDE), f32),
            pltpu.VMEM((PACKED, 128), f32),
            pltpu.VMEM((NY, ROWS, LAST), f32),
            pltpu.VMEM((NY, PACKED, 128), f32),
            pltpu.VMEM((ROWS, COLS), f32),
            pltpu.VMEM((PACKED, 128), f32),
            pltpu.VMEM((PACKED, 128), f32),
            dma((11,)),
            dma((3, 4, 2)), dma((3, 4, 2)),
            dma((7,)), dma((7,)),
            dma((7,)), dma((7,)),
            dma((12,)), dma((12,)),
            dma((2, 8)), dma((2, 8)), dma((7,)), dma((7,)),
            dma((2, 8)), dma((2, 8)), dma((7,)), dma((7,)),
            dma((2, 8)), dma((2, 8)), dma((8,)), dma((8,)),
            dma((2, 8)), dma((8,)),
        ],
        compiler_params=pltpu.CompilerParams(
            collective_id=0, has_side_effects=True, vmem_limit_bytes=62 * 2**20
        ),
        cost_estimate=pl.CostEstimate(
            flops=2 * SET * 4 * (DEPTH + ROWS) * COLS,
            bytes_accessed=8 * 2**20, transcendentals=0,
        ),
    )(
        amplitudes, integrals.T, hole_ints, driver, e_occ.reshape(1, 128),
        e_virt.reshape(1, 288), occ_pairs, virt_pairs,
    )
    tall = 16
    return pl.pallas_call(
        place_kernel,
        grid=(ROWS // tall,),
        out_shape=jax.ShapeDtypeStruct((ROWS, VP), f32),
        in_specs=[
            pl.BlockSpec((2 * NY, tall, LAST), lambda i: (0, i, 0)),
            pl.BlockSpec((2 * NY, PACKED, 128), lambda i: (0, 0, 0)),
        ],
        out_specs=pl.BlockSpec((tall, VP), lambda i: (i, 0)),
        scratch_shapes=[pltpu.VMEM((2 * NY, ROWS, 128), f32)],
        compiler_params=pltpu.CompilerParams(vmem_limit_bytes=62 * 2**20),
    )(blocks, last)


def solution(mesh):
    placed = (
        P("pair", None),
        P("pair", "grp"),
        P(),
        P("pair", "grp"),
        P(),
        P(),
        P(None, "pair"),
        P(None, "grp"),
    )
    return jax.shard_map(
        shards, mesh=mesh, in_specs=placed, out_specs=P("pair", None), check_vma=False
    )
```

```python
import jax
import jax.numpy as jnp
from jax import lax
from jax.experimental import pallas as pl
from jax.experimental.pallas import tpu as pltpu
from jax.sharding import PartitionSpec as P

MESH = pl.DeviceIdType.MESH
NX, NY, NZ = 4, 8, 8
ROWS = 64
SET = NZ * ROWS
DEPTH = 324
COLS = 648
LANES = 384
FRAME = 768
DEEP = NX * LANES
TALL = 656
VP = 10368
WIDE = 256
LAST = 2 * WIDE
REST = COLS - LAST - 128
PACKED = ROWS + REST
TILED = 80
TOP = 32767.0
TINY = 1e-33
FAR = (4, 3, 5, 2, 6, 1, 7)


def ladder_kernel(
    amp, ints, holes, drv, eocc, evirt, opairs, vpairs, out, out_last, out_scale,
    amp_in, ints_in, drv_in, hole_win, eocc_in, evirt_in, opairs_in, vpairs_in,
    own_vt, vt, ra, ap, al, hole_rel, part, part_last, via3, via3_last, via4, via4_last, rs, rs_last,
    scale, fr, fr_last, fr_scale, gap, gap_last, drv_last,
    in_sem, x_send, x_recv, a_send, a_recv, ay_send, ay_recv, ad_send, ad_recv,
    z_send, z_recv, y_send, y_recv, c_send, c_recv, o_sem,
):
    grp, pair = lax.axis_index("grp"), lax.axis_index("pair")
    y, core = grp // 2, lax.rem(grp, 2)
    x, z = pair // NZ, lax.rem(pair, NZ)

    def at_x(d):
        return (grp, lax.rem(x + d, NX) * NZ + z)

    def at_z(d):
        return (grp, x * NZ + lax.rem(z + d, NZ))

    def at_y(d):
        return (lax.rem(y + d, NY) * 2 + core, pair)

    sibling = (y * 2 + 1 - core, pair)

    barrier = pltpu.get_barrier_semaphore()
    peers = [at_x(d) for d in (1, 2, 3)] + [at_z(d) for d in FAR]
    peers += [at_y(d) for d in FAR] + [sibling]
    for peer in peers:
        pl.semaphore_signal(barrier, inc=1, device_id=peer, device_id_type=MESH)

    loads = [
        pltpu.make_async_copy(ints, ints_in, in_sem.at[0]),
        pltpu.make_async_copy(amp, amp_in, in_sem.at[1]),
        pltpu.make_async_copy(drv, drv_in, in_sem.at[2]),
        pltpu.make_async_copy(eocc, eocc_in, in_sem.at[3]),
        pltpu.make_async_copy(evirt, evirt_in, in_sem.at[4]),
        pltpu.make_async_copy(opairs, opairs_in, in_sem.at[5]),
        pltpu.make_async_copy(vpairs, vpairs_in, in_sem.at[6]),
    ]
    for k in range(NX):
        rows = pl.ds(pl.multiple_of(x * SET, SET), SET)
        cols = pl.ds(pl.multiple_of((k * NZ + z) // 2 * 128, 128), 128)
        loads.append(
            pltpu.make_async_copy(
                holes.at[rows, cols], hole_win.at[:, pl.ds(128 * k, 128)], in_sem.at[7 + k]
            )
        )
    for load in loads:
        load.start()

    half = pl.multiple_of(lax.rem(z, 2) * ROWS, ROWS)
    other = pl.multiple_of(ROWS - lax.rem(z, 2) * ROWS, ROWS)
    started = []

    def send(src, dst, send_sem, recv_sem, device):
        copy = pltpu.make_async_remote_copy(
            src_ref=src, dst_ref=dst, send_sem=send_sem, recv_sem=recv_sem,
            device_id=device, device_id_type=MESH,
        )
        copy.start()
        started.append(copy)
        return copy

    loads[0].wait()
    own_vt[COLS:TALL, :] = jnp.zeros((TALL - COLS, LANES), jnp.bfloat16)
    own_vt[0:COLS, 256:LANES] = jnp.zeros((COLS, LANES - 256), jnp.bfloat16)
    own_vt[0:COLS, 0:DEPTH] = ints_in[...]

    loads[1].wait()
    start = pl.multiple_of(grp * (COLS // 128) * 128, 128)
    window = amp_in[:, pl.ds(start, FRAME)].astype(jnp.float32)
    window = pltpu.roll(window, lax.rem(FRAME - grp * (COLS % 128), FRAME), axis=1)
    for k in range(NX):
        ra[pl.ds(128 * k + other, ROWS), :] = jnp.zeros((ROWS, FRAME), jnp.bfloat16)
    ra[pl.ds(128 * x + half, ROWS), :] = window.astype(jnp.bfloat16)

    for k in range(NX):
        for t in range(NZ):
            first = (k * NZ + t) * DEPTH
            at = k * LANES
            ap[t, :, at + 256 : at + LANES] = jnp.zeros((ROWS, LANES - 256), jnp.bfloat16)
            ap[t, :, at : at + DEPTH] = amp_in[:, first : first + DEPTH]

    pl.semaphore_wait(barrier, len(peers))

    both = pl.ds(pl.multiple_of(core * 2 * LANES, 128), 2 * LANES)

    def unit_of(chip):
        rows = pl.ds(pl.multiple_of(lax.rem(chip, 2) * 32 + core * 16, 16), 16)
        return rows, pl.ds(pl.multiple_of(chip // 2 * LANES, 128), LANES)

    rows, lanes = unit_of(y)
    far_copies = [
        send(ap.at[lax.rem(z + d, NZ), rows, lanes], al.at[NZ - d, rows, lanes],
             a_send.at[d - 1], a_recv.at[d - 1], at_z(d))
        for d in (4, 3, 5)
    ]

    def x_sends(c, owner, d, slot, side=None):
        first, tall, wide = c * WIDE, (TALL - LAST if c == 2 else WIDE), WIDE
        if side is not None:
            first, tall, wide = first + 128 * side, 128, 128
        to = vt.at[pl.ds(first, tall), pl.ds(pl.multiple_of(owner * LANES, 128), LANES)]
        cells = ra.at[pl.ds(pl.multiple_of(128 * owner + half, ROWS), ROWS), pl.ds(first, wide)]
        return [
            send(own_vt.at[pl.ds(first, tall)] if owner is x else to, to,
                 x_send.at[c, slot, 0], x_recv.at[c, slot, 0], at_x(d)),
            send(cells, cells, x_send.at[c, slot, 1], x_recv.at[c, slot, 1], at_x(d)),
        ]

    x_copies = [[], [], []]

    def x_first(c):
        x_copies[c] = [x_sends(c, x, 1, 0), x_sends(c, x, 3, 1)]

    def x_second(c):
        for copies in x_copies[c]:
            for copy in copies:
                copy.wait_recv()
        x_copies[c] = [
            x_sends(c, lax.rem(x + 3, NX), 1, 2, 0),
            x_sends(c, lax.rem(x + 1, NX), 3, 3, 1),
        ]

    x_first(0)
    near_copies = [
        send(ap.at[lax.rem(z + d, NZ), :, both], al.at[NZ - d, :, both],
             a_send.at[d - 1], a_recv.at[d - 1], at_z(d))
        for d in (2, 6, 1, 7)
    ]
    x_first(1)

    vt[:, pl.ds(pl.multiple_of(x * LANES, 128), LANES)] = own_vt[...]
    al[0] = ap[z]

    for load in loads[2:]:
        load.wait()
    orbital = lax.broadcasted_iota(jnp.int32, (128, 128), 0)
    diagonal = orbital == lax.broadcasted_iota(jnp.int32, (128, 128), 1)

    def column(row):
        spread = jnp.where(diagonal, jnp.broadcast_to(row, (128, 128)), 0.0)
        return jnp.sum(spread, axis=1, keepdims=True)

    occ = column(eocc_in[...])
    hole_row = jnp.zeros((1, ROWS), jnp.float32)
    for s in range(2):
        labels = jnp.broadcast_to(opairs_in[s : s + 1, :], (128, ROWS))
        table = lax.broadcasted_iota(jnp.int32, (128, ROWS), 0)
        picked = jnp.where(labels == table, jnp.broadcast_to(occ, (128, ROWS)), 0.0)
        hole_row = hole_row + jnp.sum(picked, axis=0, keepdims=True)
    square = lax.broadcasted_iota(jnp.int32, (ROWS, ROWS), 0)
    square = square == lax.broadcasted_iota(jnp.int32, (ROWS, ROWS), 1)
    hole_col = jnp.sum(
        jnp.where(square, jnp.broadcast_to(hole_row, (ROWS, ROWS)), 0.0),
        axis=1, keepdims=True,
    )
    padded = jnp.concatenate([evirt_in[...].reshape(1, 288), jnp.zeros((1, 96), jnp.float32)], axis=1)
    virts = [column(padded[:, 128 * b : 128 * b + 128]) for b in range(3)]
    pair_row = jnp.zeros((1, COLS), jnp.float32)
    for s in range(2):
        labels = jnp.broadcast_to(vpairs_in[s : s + 1, :], (128, COLS))
        table = lax.broadcasted_iota(jnp.int32, (128, COLS), 0)
        picked = jnp.zeros((128, COLS), jnp.float32)
        for b in range(3):
            virt = jnp.broadcast_to(virts[b], (128, COLS))
            picked = jnp.where(labels == table + 128 * b, virt, picked)
        pair_row = pair_row + jnp.sum(picked, axis=0, keepdims=True)
    gap[...] = pair_row - hole_col

    def turned(block):
        tile = jnp.concatenate([block, jnp.zeros((ROWS, 128 - REST), jnp.float32)], axis=1)
        tile = jnp.concatenate([tile, jnp.zeros((128 - ROWS, 128), jnp.float32)], axis=0)
        return jnp.transpose(tile)[0:REST, 0:ROWS]

    gap_last[...] = jnp.ones(gap_last.shape, jnp.float32)
    gap_last[0:ROWS, :] = gap[:, LAST : LAST + 128]
    gap_last[ROWS:PACKED, 0:ROWS] = turned(gap[:, COLS - REST : COLS])
    drv_last[...] = jnp.zeros(drv_last.shape, jnp.float32)
    drv_last[0:ROWS, :] = drv_in[:, LAST : LAST + 128].astype(jnp.float32)
    drv_last[ROWS:PACKED, 0:ROWS] = turned(drv_in[:, COLS - REST : COLS].astype(jnp.float32))

    for r in range(NZ):
        lines = pl.ds(pl.multiple_of(lax.rem(z + r, NZ) * ROWS, ROWS), ROWS)
        hole_rel[r * ROWS : (r + 1) * ROWS, :] = hole_win[lines, :]

    ad_copies = []

    def share(ref, slot):
        ad_copies.append(send(ref, ref, ad_send.at[slot], ad_recv.at[slot], sibling))

    far = pl.ds(3, 3)
    for copy in far_copies:
        copy.wait_recv()
    own = al.at[far, rows, lanes]
    ay_copies = [
        send(own, own, ay_send.at[d - 1], ay_recv.at[d - 1], at_y(d)) for d in FAR
    ]
    share(own, 0)
    x_second(0)
    x_copies[2] = [x_sends(2, x, d, d - 1) for d in (2, 1, 3)]
    for slot, (copy, d) in enumerate(zip(near_copies, (2, 6, 1, 7))):
        copy.wait_recv()
        share(al.at[NZ - d, :, both], 8 + slot)
    x_second(1)
    for copy, d in zip(ay_copies, FAR):
        copy.wait_recv()
        rows, lanes = unit_of(lax.rem(y + NY - d, NY))
        share(al.at[far, rows, lanes], d)
    for copy in ad_copies:
        copy.wait_recv()

    def product(c):
        first, tall = c * WIDE, (TALL - LAST if c == 2 else WIDE)
        for copies in x_copies[c]:
            for copy in copies:
                copy.wait_recv()
        return lax.dot_general(
            al[...].reshape(SET, DEEP), vt[first : first + tall, :],
            (((1,), (1,)), ((), ())), preferred_element_type=jnp.float32,
        ) + jnp.dot(
            hole_rel[...], ra[:, first : first + tall], preferred_element_type=jnp.float32
        )

    z_copies, z_later, y_copies = [None] * 3, [None] * 3, [None] * 3
    c_copies, o_copies = [], []

    sums = (part.at[0], part.at[1], part_last)
    via_3 = (via3.at[0], via3.at[1], via3_last)
    via_4 = (via4.at[0], via4.at[1], via4_last)
    landed = (rs.at[0], rs.at[1], rs_last)

    def sides(c):
        if c < 2:
            return (slice(0, ROWS), slice(0, 128)), (slice(0, ROWS), slice(128, 256))
        return (slice(0, 40), slice(0, 128)), (slice(40, PACKED), slice(0, 128))

    def z_send_to(c, i, src, dst, d):
        return send(src, dst, z_send.at[c, i], z_recv.at[c, i], at_z(d))

    def z_first(c):
        a, b = sides(c)
        at_b = (slice(0, PACKED - 40), slice(0, 128)) if c == 2 else (slice(0, ROWS), slice(0, 128))
        z_copies[c] = [
            z_send_to(c, 0, sums[c].at[(4,) + a], via_4[c].at[0], 2),
            z_send_to(c, 1, sums[c].at[(4,) + b], via_4[c].at[(1,) + at_b], 6),
            z_send_to(c, 2, sums[c].at[3], via_3[c].at[0], 1),
            z_send_to(c, 3, sums[c].at[5], via_3[c].at[1], 7),
        ]

    def z_direct(c):
        z_later[c] = [
            z_send_to(c, 4, sums[c].at[1], landed[c].at[0], 1),
            z_send_to(c, 5, sums[c].at[7], landed[c].at[1], 7),
        ]

    def relay(c):
        for copy in z_copies[c]:
            copy.wait_recv()
        a, b = sides(c)
        at_b = (slice(0, PACKED - 40), slice(0, 128)) if c == 2 else (slice(0, ROWS), slice(0, 128))
        store = sums[c]
        store[2] = store[2] + via_3[c][0]
        store[(2,) + a] = store[(2,) + a] + via_4[c][0]
        store[6] = store[6] + via_3[c][1]
        store[(6,) + b] = store[(6,) + b] + via_4[c][(1,) + at_b]
        z_later[c] += [
            z_send_to(c, 6, store.at[2], landed[c].at[2], 2),
            z_send_to(c, 7, store.at[6], landed[c].at[3], 6),
        ]

    def summed(c):
        for copy in z_later[c]:
            copy.wait_recv()
        got = landed[c]
        return sums[c][0] + ((got[0] + got[1]) + (got[2] + got[3]))

    def multiply(c):
        part[c] = product(c).reshape(NZ, ROWS, WIDE)
        z_first(c)

    def multiply_last():
        total = product(2)
        part_last[:, 0:ROWS, :] = total[:, 0:128].reshape(NZ, ROWS, 128)
        rest = jnp.concatenate(
            [total[:, 128:144], jnp.zeros((SET, 112), jnp.float32)], axis=1
        )
        for b in range(SET // 128):
            tile = jnp.transpose(rest[128 * b : 128 * b + 128])[0:REST]
            part_last[2 * b, ROWS:PACKED, 0:ROWS] = tile[:, 0:ROWS]
            part_last[2 * b + 1, ROWS:PACKED, 0:ROWS] = tile[:, ROWS : 2 * ROWS]
        z_first(2)

    def code(values, tile, rows):
        most = jnp.maximum(jnp.max(jnp.abs(values), axis=0, keepdims=True), TINY)
        scale[tile : tile + 1, :] = most * (1.0 / TOP)
        codes = jnp.round(values * (TOP / most)).astype(jnp.int32)
        if rows > values.shape[0]:
            codes = jnp.concatenate(
                [codes, jnp.zeros((rows - values.shape[0], 128), jnp.int32)], axis=0
            )
        return codes.astype(jnp.int16)

    turn = grp * (COLS % 128)

    def update(c):
        first = c * WIDE
        total = summed(c)
        driver = drv_in[:, first : first + WIDE].astype(jnp.float32)
        total = (driver + total) / gap[:, first : first + WIDE]
        for j in range(2):
            tile = pltpu.roll(total[:, 128 * j : 128 * j + 128], turn, axis=1)
            lanes = slice(first + 128 * j, first + 128 * j + 128)
            fr[y, :, lanes] = code(tile, 2 * c + j, ROWS)
        cols = pl.ds(first, WIDE)
        y_copies[c] = [
            send(fr.at[y, :, cols], fr.at[y, :, cols], y_send.at[c, d - 1], y_recv.at[c, d - 1], at_y(d))
            for d in FAR
        ]
        cross(fr.at[y, :, cols], out.at[y, core, :, cols], c, 0)

    def cross(src, dst, kind, d):
        c_copies.append(send(src, dst, c_send.at[kind, d], c_recv.at[kind, d], sibling))

    def spread(c):
        cols = pl.ds(c * WIDE, WIDE)
        for copy, d in zip(y_copies[c], FAR):
            copy.wait_recv()
            owner = lax.rem(y + NY - d, NY)
            cross(fr.at[owner, :, cols], out.at[owner, core, :, cols], c, d)
        copy = pltpu.make_async_copy(fr.at[:, :, cols], out.at[:, core, :, cols], o_sem.at[c])
        copy.start()
        o_copies.append(copy)

    def update_last():
        total = (drv_last[...] + summed(2)) / gap_last[...]
        total = jnp.concatenate(
            [pltpu.roll(total[0:ROWS], turn, axis=1), total[ROWS:PACKED]], axis=0
        )
        fr_last[y] = code(total, 4, TILED)
        fr_scale[y] = scale[...]
        copies = []
        for d in FAR:
            for i, ref in enumerate((fr_scale.at[y], fr_last.at[y])):
                copies.append(
                    send(ref, ref, y_send.at[2 + i, d - 1], y_recv.at[2 + i, d - 1], at_y(d))
                )
        cross(fr_scale.at[y], out_scale.at[y, core], 2, 0)
        cross(fr_last.at[y], out_last.at[y, core], 3, 0)
        return copies

    def spread_last(copies):
        for i, d in enumerate(FAR):
            owner = lax.rem(y + NY - d, NY)
            copies[2 * i].wait_recv()
            cross(fr_scale.at[owner], out_scale.at[owner, core], 2, d)
            copies[2 * i + 1].wait_recv()
            cross(fr_last.at[owner], out_last.at[owner, core], 3, d)
        for kind, (src, dst) in enumerate(((fr_scale, out_scale), (fr_last, out_last))):
            copy = pltpu.make_async_copy(src, dst.at[:, core], o_sem.at[2 + kind])
            copy.start()
            o_copies.append(copy)

    scale[...] = jnp.zeros(scale.shape, jnp.float32)
    part_last[:, ROWS:PACKED, :] = jnp.zeros((NZ, REST, 128), jnp.float32)
    multiply(0)
    multiply(1)
    z_direct(0)
    relay(0)
    multiply_last()
    z_direct(1)
    relay(1)
    z_direct(2)
    update(0)
    relay(2)
    update(1)
    last = update_last()
    spread(0)
    spread(1)
    spread_last(last)
    for copy in c_copies:
        copy.wait_recv()
    for copy in o_copies:
        copy.wait()
    for copy in started:
        copy.wait_send()


def place_kernel(codes, last, scale, out):
    tall = out.shape[0]
    rows = pl.ds(pl.multiple_of(pl.program_id(0) * tall, tall), tall)
    lane = lax.broadcasted_iota(jnp.int32, (tall, 128), 1)

    def value(coded):
        return coded.astype(jnp.int32).astype(jnp.float32)

    def tile(g, j):
        at = (g // 2, g % 2)
        coded = codes[at + (slice(None), slice(128 * j, 128 * j + 128))] if j < 4 else last[at + (rows,)]
        return value(coded) * scale[at + (slice(j, j + 1),)]

    rest = [
        value(last[g // 2, g % 2, ROWS:TILED, :])[0:REST] * scale[g // 2, g % 2, 4:5, :]
        for g in range(2 * NY)
    ]
    rest = jnp.transpose(jnp.concatenate(rest, axis=0))
    rest = rest[0:ROWS].reshape(ROWS // tall, tall, 128)
    step = pl.program_id(0)
    mine = rest[0]
    for i in range(1, ROWS // tall):
        mine = jnp.where(step == i, rest[i], mine)

    before = None
    for g in range(2 * NY):
        edge = REST * g
        for j in range(5):
            now = tile(g, j)
            first = 128 * (5 * g + j)
            out[:, first : first + 128] = now if before is None else jnp.where(lane < edge, before, now)
            before = now
        before = jnp.where(lane < edge, before, mine)
    out[:, VP - 128 : VP] = before


def shards(amplitudes, integrals, hole_ints, driver, e_occ, e_virt, occ_pairs, virt_pairs):
    dma = pltpu.SemaphoreType.DMA
    bf16, f32, i16 = jnp.bfloat16, jnp.float32, jnp.int16
    codes, last, scale = pl.pallas_call(
        ladder_kernel,
        out_shape=[
            jax.ShapeDtypeStruct((NY, 2, ROWS, LAST), i16),
            jax.ShapeDtypeStruct((NY, 2, TILED, 128), i16),
            jax.ShapeDtypeStruct((NY, 2, 8, 128), f32),
        ],
        in_specs=[pl.BlockSpec(memory_space=pl.ANY)] * 8,
        out_specs=[pl.BlockSpec(memory_space=pl.ANY)] * 3,
        scratch_shapes=[
            pltpu.VMEM((ROWS, VP), bf16),
            pltpu.VMEM((COLS, DEPTH), bf16),
            pltpu.VMEM((ROWS, COLS), bf16),
            pltpu.VMEM((SET, NX * 128), bf16),
            pltpu.VMEM((1, 128), f32),
            pltpu.VMEM((288,), f32),
            pltpu.VMEM((2, ROWS), jnp.int32),
            pltpu.VMEM((2, COLS), jnp.int32),
            pltpu.VMEM((TALL, LANES), bf16),
            pltpu.VMEM((TALL, DEEP), bf16),
            pltpu.VMEM((NX * 128, FRAME), bf16),
            pltpu.VMEM((NZ, ROWS, DEEP), bf16),
            pltpu.VMEM((NZ, ROWS, DEEP), bf16),
            pltpu.VMEM((SET, NX * 128), bf16),
            pltpu.VMEM((2, NZ, ROWS, WIDE), f32),
            pltpu.VMEM((NZ, PACKED, 128), f32),
            pltpu.VMEM((2, 2, ROWS, WIDE), f32),
            pltpu.VMEM((2, PACKED, 128), f32),
            pltpu.VMEM((2, 2, ROWS, 128), f32),
            pltpu.VMEM((2, 40, 128), f32),
            pltpu.VMEM((2, 4, ROWS, WIDE), f32),
            pltpu.VMEM((4, PACKED, 128), f32),
            pltpu.VMEM((8, 128), f32),
            pltpu.VMEM((NY, ROWS, LAST), i16),
            pltpu.VMEM((NY, TILED, 128), i16),
            pltpu.VMEM((NY, 8, 128), f32),
            pltpu.VMEM((ROWS, COLS), f32),
            pltpu.VMEM((PACKED, 128), f32),
            pltpu.VMEM((PACKED, 128), f32),
            dma((11,)),
            dma((3, 4, 2)), dma((3, 4, 2)),
            dma((7,)), dma((7,)),
            dma((7,)), dma((7,)),
            dma((12,)), dma((12,)),
            dma((3, 8)), dma((3, 8)),
            dma((4, 7)), dma((4, 7)),
            dma((4, 8)), dma((4, 8)),
            dma((4,)),
        ],
        compiler_params=pltpu.CompilerParams(
            collective_id=0, has_side_effects=True, vmem_limit_bytes=62 * 2**20
        ),
        cost_estimate=pl.CostEstimate(
            flops=2 * SET * 4 * (DEPTH + ROWS) * COLS,
            bytes_accessed=8 * 2**20, transcendentals=0,
        ),
    )(
        amplitudes, integrals.T, hole_ints, driver, e_occ.reshape(1, 128),
        e_virt, occ_pairs, virt_pairs,
    )
    tall = 16
    return pl.pallas_call(
        place_kernel,
        grid=(ROWS // tall,),
        out_shape=jax.ShapeDtypeStruct((ROWS, VP), f32),
        in_specs=[
            pl.BlockSpec((NY, 2, tall, LAST), lambda i: (0, 0, i, 0)),
            pl.BlockSpec((NY, 2, TILED, 128), lambda i: (0, 0, 0, 0)),
            pl.BlockSpec((NY, 2, 8, 128), lambda i: (0, 0, 0, 0)),
        ],
        out_specs=pl.BlockSpec((tall, VP), lambda i: (i, 0)),
        compiler_params=pltpu.CompilerParams(vmem_limit_bytes=62 * 2**20),
    )(codes, last, scale)


def solution(mesh):
    placed = (
        P("pair", None),
        P("pair", "grp"),
        P(),
        P("pair", "grp"),
        P(),
        P(),
        P(None, "pair"),
        P(None, "grp"),
    )
    return jax.shard_map(
        shards, mesh=mesh, in_specs=placed, out_specs=P("pair", None), check_vma=False
    )
```

```python
import jax
import jax.numpy as jnp
from jax import lax
from jax.experimental import pallas as pl
from jax.experimental.pallas import tpu as pltpu
from jax.sharding import PartitionSpec as P

MESH = pl.DeviceIdType.MESH
NX, NY, NZ = 4, 8, 8
ROWS = 64
SET = NZ * ROWS
DEPTH = 324
COLS = 648
LANES = 384
FRAME = 768
DEEP = NX * LANES
TALL = 656
VP = 10368
WIDE = 256
LAST = 2 * WIDE
REST = COLS - LAST - 128
PACKED = ROWS + REST
TILED = 80
TOP = 32767.0
TINY = 1e-33
FAR = (4, 3, 5, 2, 6, 1, 7)


def ladder_kernel(
    amp, ints, holes, drv, eocc, evirt, opairs, vpairs, out, out_last, out_scale,
    amp_in, ints_in, drv_in, hole_win, eocc_in, evirt_in, opairs_in, vpairs_in,
    own_vt, vt, ra, ap, al, hole_rel, part, part_last, via3, via3_last, via4, via4_last, rs, rs_last,
    scale, fr, fr_last, fr_scale, gap, gap_last, drv_last,
    in_sem, x_send, x_recv, a_send, a_recv, ay_send, ay_recv, ad_send, ad_recv,
    z_send, z_recv, y_send, y_recv, c_send, c_recv, o_sem,
):
    grp, pair = lax.axis_index("grp"), lax.axis_index("pair")
    y, core = grp // 2, lax.rem(grp, 2)
    x, z = pair // NZ, lax.rem(pair, NZ)

    def at_x(d):
        return (grp, lax.rem(x + d, NX) * NZ + z)

    def at_z(d):
        return (grp, x * NZ + lax.rem(z + d, NZ))

    def at_y(d):
        return (lax.rem(y + d, NY) * 2 + core, pair)

    sibling = (y * 2 + 1 - core, pair)

    barrier = pltpu.get_barrier_semaphore()
    peers = [at_x(d) for d in (1, 2, 3)] + [at_z(d) for d in FAR]
    peers += [at_y(d) for d in FAR] + [sibling]
    for peer in peers:
        pl.semaphore_signal(barrier, inc=1, device_id=peer, device_id_type=MESH)

    loads = [
        pltpu.make_async_copy(ints, ints_in, in_sem.at[0]),
        pltpu.make_async_copy(amp, amp_in, in_sem.at[1]),
        pltpu.make_async_copy(drv, drv_in, in_sem.at[2]),
        pltpu.make_async_copy(eocc, eocc_in, in_sem.at[3]),
        pltpu.make_async_copy(evirt, evirt_in, in_sem.at[4]),
        pltpu.make_async_copy(opairs, opairs_in, in_sem.at[5]),
        pltpu.make_async_copy(vpairs, vpairs_in, in_sem.at[6]),
    ]
    for k in range(NX):
        rows = pl.ds(pl.multiple_of(x * SET, SET), SET)
        cols = pl.ds(pl.multiple_of((k * NZ + z) // 2 * 128, 128), 128)
        loads.append(
            pltpu.make_async_copy(
                holes.at[rows, cols], hole_win.at[:, pl.ds(128 * k, 128)], in_sem.at[7 + k]
            )
        )
    for load in loads:
        load.start()

    half = pl.multiple_of(lax.rem(z, 2) * ROWS, ROWS)
    other = pl.multiple_of(ROWS - lax.rem(z, 2) * ROWS, ROWS)
    started = []

    def send(src, dst, send_sem, recv_sem, device):
        copy = pltpu.make_async_remote_copy(
            src_ref=src, dst_ref=dst, send_sem=send_sem, recv_sem=recv_sem,
            device_id=device, device_id_type=MESH,
        )
        copy.start()
        started.append(copy)
        return copy

    loads[0].wait()
    own_vt[COLS:TALL, :] = jnp.zeros((TALL - COLS, LANES), jnp.bfloat16)
    own_vt[0:COLS, 256:LANES] = jnp.zeros((COLS, LANES - 256), jnp.bfloat16)
    own_vt[0:COLS, 0:DEPTH] = ints_in[...]

    loads[1].wait()
    start = pl.multiple_of(grp * (COLS // 128) * 128, 128)
    window = amp_in[:, pl.ds(start, FRAME)].astype(jnp.float32)
    window = pltpu.roll(window, lax.rem(FRAME - grp * (COLS % 128), FRAME), axis=1)
    for k in range(NX):
        ra[pl.ds(128 * k + other, ROWS), :] = jnp.zeros((ROWS, FRAME), jnp.bfloat16)
    ra[pl.ds(128 * x + half, ROWS), :] = window.astype(jnp.bfloat16)

    for k in range(NX):
        for t in range(NZ):
            first = (k * NZ + t) * DEPTH
            at = k * LANES
            ap[t, :, at + 256 : at + LANES] = jnp.zeros((ROWS, LANES - 256), jnp.bfloat16)
            ap[t, :, at : at + DEPTH] = amp_in[:, first : first + DEPTH]

    pl.semaphore_wait(barrier, len(peers))

    both = pl.ds(pl.multiple_of(core * 2 * LANES, 128), 2 * LANES)

    def unit_of(chip):
        rows = pl.ds(pl.multiple_of(lax.rem(chip, 2) * 32 + core * 16, 16), 16)
        return rows, pl.ds(pl.multiple_of(chip // 2 * LANES, 128), LANES)

    rows, lanes = unit_of(y)
    far_copies = [
        send(ap.at[lax.rem(z + d, NZ), rows, lanes], al.at[NZ - d, rows, lanes],
             a_send.at[d - 1], a_recv.at[d - 1], at_z(d))
        for d in (4, 3, 5)
    ]

    def x_sends(c, owner, d, slot, side=None):
        first, tall, wide = c * WIDE, (TALL - LAST if c == 2 else WIDE), WIDE
        if side is not None:
            first, tall, wide = first + 128 * side, 128, 128
        to = vt.at[pl.ds(first, tall), pl.ds(pl.multiple_of(owner * LANES, 128), LANES)]
        cells = ra.at[pl.ds(pl.multiple_of(128 * owner + half, ROWS), ROWS), pl.ds(first, wide)]
        return [
            send(own_vt.at[pl.ds(first, tall)] if owner is x else to, to,
                 x_send.at[c, slot, 0], x_recv.at[c, slot, 0], at_x(d)),
            send(cells, cells, x_send.at[c, slot, 1], x_recv.at[c, slot, 1], at_x(d)),
        ]

    x_copies = [[], [], []]

    def x_first(c):
        x_copies[c] = [x_sends(c, x, 1, 0), x_sends(c, x, 3, 1)]

    def x_second(c):
        for copies in x_copies[c]:
            for copy in copies:
                copy.wait_recv()
        x_copies[c] = [
            x_sends(c, lax.rem(x + 3, NX), 1, 2, 0),
            x_sends(c, lax.rem(x + 1, NX), 3, 3, 1),
        ]

    x_first(0)
    near_copies = [
        send(ap.at[lax.rem(z + d, NZ), :, both], al.at[NZ - d, :, both],
             a_send.at[d - 1], a_recv.at[d - 1], at_z(d))
        for d in (2, 6, 1, 7)
    ]
    x_first(1)

    vt[:, pl.ds(pl.multiple_of(x * LANES, 128), LANES)] = own_vt[...]
    al[0] = ap[z]

    for load in loads[2:]:
        load.wait()
    orbital = lax.broadcasted_iota(jnp.int32, (128, 128), 0)
    diagonal = orbital == lax.broadcasted_iota(jnp.int32, (128, 128), 1)

    def column(row):
        spread = jnp.where(diagonal, jnp.broadcast_to(row, (128, 128)), 0.0)
        return jnp.sum(spread, axis=1, keepdims=True)

    occ = column(eocc_in[...])
    hole_row = jnp.zeros((1, ROWS), jnp.float32)
    for s in range(2):
        labels = jnp.broadcast_to(opairs_in[s : s + 1, :], (128, ROWS))
        table = lax.broadcasted_iota(jnp.int32, (128, ROWS), 0)
        picked = jnp.where(labels == table, jnp.broadcast_to(occ, (128, ROWS)), 0.0)
        hole_row = hole_row + jnp.sum(picked, axis=0, keepdims=True)
    square = lax.broadcasted_iota(jnp.int32, (ROWS, ROWS), 0)
    square = square == lax.broadcasted_iota(jnp.int32, (ROWS, ROWS), 1)
    hole_col = jnp.sum(
        jnp.where(square, jnp.broadcast_to(hole_row, (ROWS, ROWS)), 0.0),
        axis=1, keepdims=True,
    )
    padded = jnp.concatenate([evirt_in[...].reshape(1, 288), jnp.zeros((1, 96), jnp.float32)], axis=1)
    virts = [column(padded[:, 128 * b : 128 * b + 128]) for b in range(3)]
    pair_row = jnp.zeros((1, COLS), jnp.float32)
    for s in range(2):
        labels = jnp.broadcast_to(vpairs_in[s : s + 1, :], (128, COLS))
        table = lax.broadcasted_iota(jnp.int32, (128, COLS), 0)
        picked = jnp.zeros((128, COLS), jnp.float32)
        for b in range(3):
            virt = jnp.broadcast_to(virts[b], (128, COLS))
            picked = jnp.where(labels == table + 128 * b, virt, picked)
        pair_row = pair_row + jnp.sum(picked, axis=0, keepdims=True)
    gap[...] = pair_row - hole_col

    def turned(block):
        tile = jnp.concatenate([block, jnp.zeros((ROWS, 128 - REST), jnp.float32)], axis=1)
        tile = jnp.concatenate([tile, jnp.zeros((128 - ROWS, 128), jnp.float32)], axis=0)
        return jnp.transpose(tile)[0:REST, 0:ROWS]

    gap_last[...] = jnp.ones(gap_last.shape, jnp.float32)
    gap_last[0:ROWS, :] = gap[:, LAST : LAST + 128]
    gap_last[ROWS:PACKED, 0:ROWS] = turned(gap[:, COLS - REST : COLS])
    drv_last[...] = jnp.zeros(drv_last.shape, jnp.float32)
    drv_last[0:ROWS, :] = drv_in[:, LAST : LAST + 128].astype(jnp.float32)
    drv_last[ROWS:PACKED, 0:ROWS] = turned(drv_in[:, COLS - REST : COLS].astype(jnp.float32))

    for r in range(NZ):
        lines = pl.ds(pl.multiple_of(lax.rem(z + r, NZ) * ROWS, ROWS), ROWS)
        hole_rel[r * ROWS : (r + 1) * ROWS, :] = hole_win[lines, :]

    ad_copies = []

    def share(ref, slot):
        ad_copies.append(send(ref, ref, ad_send.at[slot], ad_recv.at[slot], sibling))

    far = pl.ds(3, 3)
    for copy in far_copies:
        copy.wait_recv()
    own = al.at[far, rows, lanes]
    ay_copies = [
        send(own, own, ay_send.at[d - 1], ay_recv.at[d - 1], at_y(d)) for d in FAR
    ]
    share(own, 0)
    x_second(0)
    for slot, (copy, d) in enumerate(zip(near_copies, (2, 6, 1, 7))):
        copy.wait_recv()
        share(al.at[NZ - d, :, both], 8 + slot)
    x_second(1)
    x_copies[2] = [x_sends(2, x, d, d - 1) for d in (2, 1, 3)]
    for copy, d in zip(ay_copies, FAR):
        copy.wait_recv()
        rows, lanes = unit_of(lax.rem(y + NY - d, NY))
        share(al.at[far, rows, lanes], d)
    for copy in ad_copies:
        copy.wait_recv()

    def product(c):
        first, tall = c * WIDE, (TALL - LAST if c == 2 else WIDE)
        for copies in x_copies[c]:
            for copy in copies:
                copy.wait_recv()
        return lax.dot_general(
            al[...].reshape(SET, DEEP), vt[first : first + tall, :],
            (((1,), (1,)), ((), ())), preferred_element_type=jnp.float32,
        ) + jnp.dot(
            hole_rel[...], ra[:, first : first + tall], preferred_element_type=jnp.float32
        )

    z_copies, z_later, y_copies = [None] * 3, [None] * 3, [None] * 3
    c_copies, o_copies = [], []

    sums = (part.at[0], part.at[1], part_last)
    via_3 = (via3.at[0], via3.at[1], via3_last)
    via_4 = (via4.at[0], via4.at[1], via4_last)
    landed = (rs.at[0], rs.at[1], rs_last)

    def sides(c):
        if c < 2:
            return (slice(0, ROWS), slice(0, 128)), (slice(0, ROWS), slice(128, 256))
        return (slice(0, 40), slice(0, 128)), (slice(40, PACKED), slice(0, 128))

    def z_send_to(c, i, src, dst, d):
        return send(src, dst, z_send.at[c, i], z_recv.at[c, i], at_z(d))

    def z_first(c):
        a, b = sides(c)
        at_b = (slice(0, PACKED - 40), slice(0, 128)) if c == 2 else (slice(0, ROWS), slice(0, 128))
        z_copies[c] = [
            z_send_to(c, 0, sums[c].at[(4,) + a], via_4[c].at[0], 2),
            z_send_to(c, 1, sums[c].at[(4,) + b], via_4[c].at[(1,) + at_b], 6),
            z_send_to(c, 2, sums[c].at[3], via_3[c].at[0], 1),
            z_send_to(c, 3, sums[c].at[5], via_3[c].at[1], 7),
        ]

    def z_direct(c):
        z_later[c] = [
            z_send_to(c, 4, sums[c].at[1], landed[c].at[0], 1),
            z_send_to(c, 5, sums[c].at[7], landed[c].at[1], 7),
        ]

    def relay(c):
        for copy in z_copies[c]:
            copy.wait_recv()
        a, b = sides(c)
        at_b = (slice(0, PACKED - 40), slice(0, 128)) if c == 2 else (slice(0, ROWS), slice(0, 128))
        store = sums[c]
        store[2] = store[2] + via_3[c][0]
        store[(2,) + a] = store[(2,) + a] + via_4[c][0]
        store[6] = store[6] + via_3[c][1]
        store[(6,) + b] = store[(6,) + b] + via_4[c][(1,) + at_b]
        z_later[c] += [
            z_send_to(c, 6, store.at[2], landed[c].at[2], 2),
            z_send_to(c, 7, store.at[6], landed[c].at[3], 6),
        ]

    def summed(c):
        for copy in z_later[c]:
            copy.wait_recv()
        got = landed[c]
        return sums[c][0] + ((got[0] + got[1]) + (got[2] + got[3]))

    def multiply(c):
        part[c] = product(c).reshape(NZ, ROWS, WIDE)
        z_first(c)

    def multiply_last():
        total = product(2)
        part_last[:, 0:ROWS, :] = total[:, 0:128].reshape(NZ, ROWS, 128)
        rest = jnp.concatenate(
            [total[:, 128:144], jnp.zeros((SET, 112), jnp.float32)], axis=1
        )
        for b in range(SET // 128):
            tile = jnp.transpose(rest[128 * b : 128 * b + 128])[0:REST]
            part_last[2 * b, ROWS:PACKED, 0:ROWS] = tile[:, 0:ROWS]
            part_last[2 * b + 1, ROWS:PACKED, 0:ROWS] = tile[:, ROWS : 2 * ROWS]
        z_first(2)

    def code(values, tile, rows):
        most = jnp.maximum(jnp.max(jnp.abs(values), axis=0, keepdims=True), TINY)
        scale[tile : tile + 1, :] = most * (1.0 / TOP)
        codes = jnp.round(values * (TOP / most)).astype(jnp.int32)
        if rows > values.shape[0]:
            codes = jnp.concatenate(
                [codes, jnp.zeros((rows - values.shape[0], 128), jnp.int32)], axis=0
            )
        return codes.astype(jnp.int16)

    turn = grp * (COLS % 128)

    def update(c):
        first = c * WIDE
        total = summed(c)
        driver = drv_in[:, first : first + WIDE].astype(jnp.float32)
        total = (driver + total) / gap[:, first : first + WIDE]
        for j in range(2):
            tile = pltpu.roll(total[:, 128 * j : 128 * j + 128], turn, axis=1)
            lanes = slice(first + 128 * j, first + 128 * j + 128)
            fr[y, :, lanes] = code(tile, 2 * c + j, ROWS)
        cols = pl.ds(first, WIDE)
        y_copies[c] = [
            send(fr.at[y, :, cols], fr.at[y, :, cols], y_send.at[c, d - 1], y_recv.at[c, d - 1], at_y(d))
            for d in FAR
        ]
        cross(fr.at[y, :, cols], out.at[y, core, :, cols], c, 0)

    def cross(src, dst, kind, d):
        c_copies.append(send(src, dst, c_send.at[kind, d], c_recv.at[kind, d], sibling))

    def spread(c):
        cols = pl.ds(c * WIDE, WIDE)
        for copy, d in zip(y_copies[c], FAR):
            copy.wait_recv()
            owner = lax.rem(y + NY - d, NY)
            cross(fr.at[owner, :, cols], out.at[owner, core, :, cols], c, d)
        copy = pltpu.make_async_copy(fr.at[:, :, cols], out.at[:, core, :, cols], o_sem.at[c])
        copy.start()
        o_copies.append(copy)

    def update_last():
        total = (drv_last[...] + summed(2)) / gap_last[...]
        total = jnp.concatenate(
            [pltpu.roll(total[0:ROWS], turn, axis=1), total[ROWS:PACKED]], axis=0
        )
        fr_last[y] = code(total, 4, TILED)
        fr_scale[y] = scale[...]
        copies = []
        for d in FAR:
            for i, ref in enumerate((fr_scale.at[y], fr_last.at[y])):
                copies.append(
                    send(ref, ref, y_send.at[2 + i, d - 1], y_recv.at[2 + i, d - 1], at_y(d))
                )
        cross(fr_scale.at[y], out_scale.at[y, core], 2, 0)
        cross(fr_last.at[y], out_last.at[y, core], 3, 0)
        return copies

    def spread_last(copies):
        for i, d in enumerate(FAR):
            owner = lax.rem(y + NY - d, NY)
            copies[2 * i].wait_recv()
            cross(fr_scale.at[owner], out_scale.at[owner, core], 2, d)
            copies[2 * i + 1].wait_recv()
            cross(fr_last.at[owner], out_last.at[owner, core], 3, d)
        for kind, (src, dst) in enumerate(((fr_scale, out_scale), (fr_last, out_last))):
            copy = pltpu.make_async_copy(src, dst.at[:, core], o_sem.at[2 + kind])
            copy.start()
            o_copies.append(copy)

    scale[...] = jnp.zeros(scale.shape, jnp.float32)
    part_last[:, ROWS:PACKED, :] = jnp.zeros((NZ, REST, 128), jnp.float32)
    multiply(0)
    multiply(1)
    z_direct(0)
    relay(0)
    multiply_last()
    z_direct(1)
    relay(1)
    z_direct(2)
    update(0)
    relay(2)
    update(1)
    last = update_last()
    spread(0)
    spread(1)
    spread_last(last)
    for copy in c_copies:
        copy.wait_recv()
    for copy in o_copies:
        copy.wait()
    for copy in started:
        copy.wait_send()


def place_kernel(codes, last, scale, out, rest):
    tall = out.shape[0]
    rows = pl.ds(pl.multiple_of(pl.program_id(0) * tall, tall), tall)
    lane = lax.broadcasted_iota(jnp.int32, (tall, 128), 1)

    def value(coded):
        return coded.astype(jnp.int32).astype(jnp.float32)

    def tile(g, j):
        at = (g // 2, g % 2)
        coded = codes[at + (slice(None), slice(128 * j, 128 * j + 128))] if j < 4 else last[at + (rows,)]
        return value(coded) * scale[at + (slice(j, j + 1),)]

    @pl.when(pl.program_id(0) == 0)
    def _():
        lines = [
            value(last[g // 2, g % 2, ROWS:TILED, :])[0:REST] * scale[g // 2, g % 2, 4:5, :]
            for g in range(2 * NY)
        ]
        rest[...] = jnp.transpose(jnp.concatenate(lines, axis=0))

    mine = rest[rows, :]
    before = None
    for g in range(2 * NY):
        edge = REST * g
        for j in range(5):
            now = tile(g, j)
            first = 128 * (5 * g + j)
            out[:, first : first + 128] = now if before is None else jnp.where(lane < edge, before, now)
            before = now
        before = jnp.where(lane < edge, before, mine)
    out[:, VP - 128 : VP] = before


def shards(amplitudes, integrals, hole_ints, driver, e_occ, e_virt, occ_pairs, virt_pairs):
    dma = pltpu.SemaphoreType.DMA
    bf16, f32, i16 = jnp.bfloat16, jnp.float32, jnp.int16
    codes, last, scale = pl.pallas_call(
        ladder_kernel,
        out_shape=[
            jax.ShapeDtypeStruct((NY, 2, ROWS, LAST), i16),
            jax.ShapeDtypeStruct((NY, 2, TILED, 128), i16),
            jax.ShapeDtypeStruct((NY, 2, 8, 128), f32),
        ],
        in_specs=[pl.BlockSpec(memory_space=pl.ANY)] * 8,
        out_specs=[pl.BlockSpec(memory_space=pl.ANY)] * 3,
        scratch_shapes=[
            pltpu.VMEM((ROWS, VP), bf16),
            pltpu.VMEM((COLS, DEPTH), bf16),
            pltpu.VMEM((ROWS, COLS), bf16),
            pltpu.VMEM((SET, NX * 128), bf16),
            pltpu.VMEM((1, 128), f32),
            pltpu.VMEM((288,), f32),
            pltpu.VMEM((2, ROWS), jnp.int32),
            pltpu.VMEM((2, COLS), jnp.int32),
            pltpu.VMEM((TALL, LANES), bf16),
            pltpu.VMEM((TALL, DEEP), bf16),
            pltpu.VMEM((NX * 128, FRAME), bf16),
            pltpu.VMEM((NZ, ROWS, DEEP), bf16),
            pltpu.VMEM((NZ, ROWS, DEEP), bf16),
            pltpu.VMEM((SET, NX * 128), bf16),
            pltpu.VMEM((2, NZ, ROWS, WIDE), f32),
            pltpu.VMEM((NZ, PACKED, 128), f32),
            pltpu.VMEM((2, 2, ROWS, WIDE), f32),
            pltpu.VMEM((2, PACKED, 128), f32),
            pltpu.VMEM((2, 2, ROWS, 128), f32),
            pltpu.VMEM((2, 40, 128), f32),
            pltpu.VMEM((2, 4, ROWS, WIDE), f32),
            pltpu.VMEM((4, PACKED, 128), f32),
            pltpu.VMEM((8, 128), f32),
            pltpu.VMEM((NY, ROWS, LAST), i16),
            pltpu.VMEM((NY, TILED, 128), i16),
            pltpu.VMEM((NY, 8, 128), f32),
            pltpu.VMEM((ROWS, COLS), f32),
            pltpu.VMEM((PACKED, 128), f32),
            pltpu.VMEM((PACKED, 128), f32),
            dma((11,)),
            dma((3, 4, 2)), dma((3, 4, 2)),
            dma((7,)), dma((7,)),
            dma((7,)), dma((7,)),
            dma((12,)), dma((12,)),
            dma((3, 8)), dma((3, 8)),
            dma((4, 7)), dma((4, 7)),
            dma((4, 8)), dma((4, 8)),
            dma((4,)),
        ],
        compiler_params=pltpu.CompilerParams(
            collective_id=0, has_side_effects=True, vmem_limit_bytes=62 * 2**20
        ),
        cost_estimate=pl.CostEstimate(
            flops=2 * SET * 4 * (DEPTH + ROWS) * COLS,
            bytes_accessed=8 * 2**20, transcendentals=0,
        ),
    )(
        amplitudes, integrals.T, hole_ints, driver, e_occ.reshape(1, 128),
        e_virt, occ_pairs, virt_pairs,
    )
    tall = 32
    return pl.pallas_call(
        place_kernel,
        grid=(ROWS // tall,),
        out_shape=jax.ShapeDtypeStruct((ROWS, VP), f32),
        in_specs=[
            pl.BlockSpec((NY, 2, tall, LAST), lambda i: (0, 0, i, 0)),
            pl.BlockSpec((NY, 2, TILED, 128), lambda i: (0, 0, 0, 0)),
            pl.BlockSpec((NY, 2, 8, 128), lambda i: (0, 0, 0, 0)),
        ],
        out_specs=pl.BlockSpec((tall, VP), lambda i: (i, 0)),
        scratch_shapes=[pltpu.VMEM((128, 128), f32)],
        compiler_params=pltpu.CompilerParams(vmem_limit_bytes=62 * 2**20),
    )(codes, last, scale)


def solution(mesh):
    placed = (
        P("pair", None),
        P("pair", "grp"),
        P(),
        P("pair", "grp"),
        P(),
        P(),
        P(None, "pair"),
        P(None, "grp"),
    )
    return jax.shard_map(
        shards, mesh=mesh, in_specs=placed, out_specs=P("pair", None), check_vma=False
    )
```

```python
import jax
import jax.numpy as jnp
from jax import lax
from jax.experimental import pallas as pl
from jax.experimental.pallas import tpu as pltpu
from jax.sharding import PartitionSpec as P

MESH = pl.DeviceIdType.MESH
NX, NY, NZ = 4, 8, 8
ROWS = 64
SET = NZ * ROWS
DEPTH = 324
COLS = 648
LANES = 384
FRAME = 768
SPARE = LANES - DEPTH
DEEP = NX * LANES
TALL = 656
VP = 10368
WIDE = 256
LAST = 2 * WIDE
REST = COLS - LAST - 128
PACKED = ROWS + REST
TILED = 80
TOP = 32767.0
TINY = 1e-33
FAR = (4, 3, 5, 2, 6, 1, 7)


def ladder_kernel(
    amp, ints, holes, drv, eocc, evirt, opairs, vpairs, out, out_last, out_scale,
    amp_in, ints_in, drv_in, hole_own, hole_win, eocc_in, evirt_in, opairs_in, vpairs_in,
    own_vt, vt, ra, ap, al, hole_rel, part, part_last, via3, via3_last, via4, via4_last, rs, rs_last,
    scale, fr, fr_last, fr_scale, gap, gap_last, drv_last,
    in_sem, x_send, x_recv, a_send, a_recv, ay_send, ay_recv, ad_send, ad_recv,
    z_send, z_recv, y_send, y_recv, c_send, c_recv, o_sem,
):
    grp, pair = lax.axis_index("grp"), lax.axis_index("pair")
    y, core = grp // 2, lax.rem(grp, 2)
    x, z = pair // NZ, lax.rem(pair, NZ)

    def at_x(d):
        return (grp, lax.rem(x + d, NX) * NZ + z)

    def at_z(d):
        return (grp, x * NZ + lax.rem(z + d, NZ))

    def at_y(d):
        return (lax.rem(y + d, NY) * 2 + core, pair)

    sibling = (y * 2 + 1 - core, pair)

    barrier = pltpu.get_barrier_semaphore()
    peers = [at_x(d) for d in (1, 2, 3)] + [at_z(d) for d in FAR]
    peers += [at_y(d) for d in FAR] + [sibling]
    for peer in peers:
        pl.semaphore_signal(barrier, inc=1, device_id=peer, device_id_type=MESH)

    loads = [
        pltpu.make_async_copy(ints, ints_in, in_sem.at[0]),
        pltpu.make_async_copy(amp, amp_in, in_sem.at[1]),
        pltpu.make_async_copy(
            holes.at[pl.ds(pl.multiple_of(pair * ROWS, ROWS), ROWS)], hole_own, in_sem.at[2]
        ),
        pltpu.make_async_copy(drv, drv_in, in_sem.at[11]),
        pltpu.make_async_copy(eocc, eocc_in, in_sem.at[3]),
        pltpu.make_async_copy(evirt, evirt_in, in_sem.at[4]),
        pltpu.make_async_copy(opairs, opairs_in, in_sem.at[5]),
        pltpu.make_async_copy(vpairs, vpairs_in, in_sem.at[6]),
    ]
    for k in range(NX):
        rows = pl.ds(pl.multiple_of(x * SET, SET), SET)
        cols = pl.ds(pl.multiple_of((k * NZ + z) // 2 * 128, 128), 128)
        loads.append(
            pltpu.make_async_copy(
                holes.at[rows, cols], hole_win.at[:, pl.ds(128 * k, 128)], in_sem.at[7 + k]
            )
        )
    for load in loads:
        load.start()

    half = lax.rem(z, 2) * ROWS + ROWS - 16
    started = []

    def send(src, dst, send_sem, recv_sem, device):
        copy = pltpu.make_async_remote_copy(
            src_ref=src, dst_ref=dst, send_sem=send_sem, recv_sem=recv_sem,
            device_id=device, device_id_type=MESH,
        )
        copy.start()
        started.append(copy)
        return copy

    loads[0].wait()
    own_vt[COLS:TALL, :] = jnp.zeros((TALL - COLS, LANES), jnp.bfloat16)
    own_vt[0:COLS, 256:LANES] = jnp.zeros((COLS, LANES - 256), jnp.bfloat16)
    own_vt[0:COLS, 0:DEPTH] = ints_in[...]

    loads[1].wait()
    start = pl.multiple_of(grp * (COLS // 128) * 128, 128)
    window = amp_in[:, pl.ds(start, FRAME)].astype(jnp.float32)
    window = pltpu.roll(window, lax.rem(FRAME - grp * (COLS % 128), FRAME), axis=1)
    row = lax.broadcasted_iota(jnp.int32, (16, FRAME), 0)
    tail = jnp.where(row < SPARE - (ROWS - 16), 0.0, window[ROWS - 16 : ROWS])
    other = ROWS * (1 - lax.rem(z, 2)) + ROWS - 16
    for k in range(NX):
        for b in range(2):
            at = 128 * k + ROWS * b
            ra[at : at + ROWS - 16, :] = jnp.zeros((ROWS - 16, FRAME), jnp.bfloat16)
        ra[pl.ds(pl.multiple_of(128 * k + other, 16), 16), :] = jnp.zeros((16, FRAME), jnp.bfloat16)
    ra[pl.ds(pl.multiple_of(128 * x + half, 16), 16), :] = tail.astype(jnp.bfloat16)
    lane = lax.broadcasted_iota(jnp.int32, (128, 128), 1)
    for b in range(FRAME // 128):
        tall = min(128, TALL - 128 * b)
        block = jnp.concatenate(
            [window[:, 128 * b : 128 * b + 128], jnp.zeros((128 - ROWS, 128), jnp.float32)], axis=0
        )
        block = pltpu.roll(jnp.transpose(block), DEPTH - 256, axis=1)[0:tall]
        lines = slice(128 * b, 128 * b + tall)
        mixed = jnp.where(
            lane[0:tall] < DEPTH - 256, own_vt[lines, 256:LANES].astype(jnp.float32), block
        )
        own_vt[lines, 256:LANES] = mixed.astype(jnp.bfloat16)

    loads[2].wait()
    for k in range(NX):
        for t in range(NZ):
            owner = k * NZ + t
            at = k * LANES
            ap[t, :, at : at + DEPTH] = amp_in[:, owner * DEPTH : (owner + 1) * DEPTH]
            ap[t, :, at + DEPTH : at + LANES] = hole_own[:, owner * ROWS : owner * ROWS + SPARE]

    pl.semaphore_wait(barrier, len(peers))

    both = pl.ds(pl.multiple_of(core * 2 * LANES, 128), 2 * LANES)

    def unit_of(chip):
        rows = pl.ds(pl.multiple_of(lax.rem(chip, 2) * 32 + core * 16, 16), 16)
        return rows, pl.ds(pl.multiple_of(chip // 2 * LANES, 128), LANES)

    rows, lanes = unit_of(y)
    far_copies = [
        send(ap.at[lax.rem(z + d, NZ), rows, lanes], al.at[NZ - d, rows, lanes],
             a_send.at[d - 1], a_recv.at[d - 1], at_z(d))
        for d in (4, 3, 5)
    ]

    def x_sends(c, owner, d, slot, side=None):
        first, tall, wide = c * WIDE, (TALL - LAST if c == 2 else WIDE), WIDE
        if side is not None:
            first, tall, wide = first + 128 * side, 128, 128
        to = vt.at[pl.ds(first, tall), pl.ds(pl.multiple_of(owner * LANES, 128), LANES)]
        cells = ra.at[pl.ds(pl.multiple_of(128 * owner + half, 16), 16), pl.ds(first, wide)]
        return [
            send(own_vt.at[pl.ds(first, tall)] if owner is x else to, to,
                 x_send.at[c, slot, 0], x_recv.at[c, slot, 0], at_x(d)),
            send(cells, cells, x_send.at[c, slot, 1], x_recv.at[c, slot, 1], at_x(d)),
        ]

    x_copies = [[], [], []]

    def x_first(c):
        x_copies[c] = [x_sends(c, x, 1, 0), x_sends(c, x, 3, 1)]

    def x_second(c):
        for copies in x_copies[c]:
            for copy in copies:
                copy.wait_recv()
        x_copies[c] = [
            x_sends(c, lax.rem(x + 3, NX), 1, 2, 0),
            x_sends(c, lax.rem(x + 1, NX), 3, 3, 1),
        ]

    x_first(0)
    near_copies = [
        send(ap.at[lax.rem(z + d, NZ), :, both], al.at[NZ - d, :, both],
             a_send.at[d - 1], a_recv.at[d - 1], at_z(d))
        for d in (2, 6, 1, 7)
    ]
    x_first(1)

    vt[:, pl.ds(pl.multiple_of(x * LANES, 128), LANES)] = own_vt[...]
    al[0] = ap[z]

    for load in loads[3:]:
        load.wait()
    orbital = lax.broadcasted_iota(jnp.int32, (128, 128), 0)
    diagonal = orbital == lax.broadcasted_iota(jnp.int32, (128, 128), 1)

    def column(row):
        spread = jnp.where(diagonal, jnp.broadcast_to(row, (128, 128)), 0.0)
        return jnp.sum(spread, axis=1, keepdims=True)

    occ = column(eocc_in[...])
    hole_row = jnp.zeros((1, ROWS), jnp.float32)
    for s in range(2):
        labels = jnp.broadcast_to(opairs_in[s : s + 1, :], (128, ROWS))
        table = lax.broadcasted_iota(jnp.int32, (128, ROWS), 0)
        picked = jnp.where(labels == table, jnp.broadcast_to(occ, (128, ROWS)), 0.0)
        hole_row = hole_row + jnp.sum(picked, axis=0, keepdims=True)
    square = lax.broadcasted_iota(jnp.int32, (ROWS, ROWS), 0)
    square = square == lax.broadcasted_iota(jnp.int32, (ROWS, ROWS), 1)
    hole_col = jnp.sum(
        jnp.where(square, jnp.broadcast_to(hole_row, (ROWS, ROWS)), 0.0),
        axis=1, keepdims=True,
    )
    padded = jnp.concatenate([evirt_in[...].reshape(1, 288), jnp.zeros((1, 96), jnp.float32)], axis=1)
    virts = [column(padded[:, 128 * b : 128 * b + 128]) for b in range(3)]
    pair_row = jnp.zeros((1, COLS), jnp.float32)
    for s in range(2):
        labels = jnp.broadcast_to(vpairs_in[s : s + 1, :], (128, COLS))
        table = lax.broadcasted_iota(jnp.int32, (128, COLS), 0)
        picked = jnp.zeros((128, COLS), jnp.float32)
        for b in range(3):
            virt = jnp.broadcast_to(virts[b], (128, COLS))
            picked = jnp.where(labels == table + 128 * b, virt, picked)
        pair_row = pair_row + jnp.sum(picked, axis=0, keepdims=True)
    gap[...] = pair_row - hole_col

    def turned(block):
        tile = jnp.concatenate([block, jnp.zeros((ROWS, 128 - REST), jnp.float32)], axis=1)
        tile = jnp.concatenate([tile, jnp.zeros((128 - ROWS, 128), jnp.float32)], axis=0)
        return jnp.transpose(tile)[0:REST, 0:ROWS]

    gap_last[...] = jnp.ones(gap_last.shape, jnp.float32)
    gap_last[0:ROWS, :] = gap[:, LAST : LAST + 128]
    gap_last[ROWS:PACKED, 0:ROWS] = turned(gap[:, COLS - REST : COLS])
    drv_last[...] = jnp.zeros(drv_last.shape, jnp.float32)
    drv_last[0:ROWS, :] = drv_in[:, LAST : LAST + 128].astype(jnp.float32)
    drv_last[ROWS:PACKED, 0:ROWS] = turned(drv_in[:, COLS - REST : COLS].astype(jnp.float32))

    for r in range(NZ):
        lines = pl.ds(pl.multiple_of(lax.rem(z + r, NZ) * ROWS, ROWS), ROWS)
        hole_rel[r * ROWS : (r + 1) * ROWS, :] = hole_win[lines, :]

    ad_copies = []

    def share(ref, slot):
        ad_copies.append(send(ref, ref, ad_send.at[slot], ad_recv.at[slot], sibling))

    far = pl.ds(3, 3)
    for copy in far_copies:
        copy.wait_recv()
    own = al.at[far, rows, lanes]
    ay_copies = [
        send(own, own, ay_send.at[d - 1], ay_recv.at[d - 1], at_y(d)) for d in FAR
    ]
    share(own, 0)
    x_second(0)
    for slot, (copy, d) in enumerate(zip(near_copies, (2, 6, 1, 7))):
        copy.wait_recv()
        share(al.at[NZ - d, :, both], 8 + slot)
    x_second(1)
    x_copies[2] = [x_sends(2, x, d, d - 1) for d in (2, 1, 3)]
    for copy, d in zip(ay_copies, FAR):
        copy.wait_recv()
        rows, lanes = unit_of(lax.rem(y + NY - d, NY))
        share(al.at[far, rows, lanes], d)
    for copy in ad_copies:
        copy.wait_recv()

    def product(c):
        first, tall = c * WIDE, (TALL - LAST if c == 2 else WIDE)
        for copies in x_copies[c]:
            for copy in copies:
                copy.wait_recv()
        return lax.dot_general(
            al[...].reshape(SET, DEEP), vt[first : first + tall, :],
            (((1,), (1,)), ((), ())), preferred_element_type=jnp.float32,
        ) + jnp.dot(
            hole_rel[...], ra[:, first : first + tall], preferred_element_type=jnp.float32
        )

    z_copies, z_later, y_copies = [None] * 3, [None] * 3, [None] * 3
    c_copies, o_copies = [], []

    sums = (part.at[0], part.at[1], part_last)
    via_3 = (via3.at[0], via3.at[1], via3_last)
    via_4 = (via4.at[0], via4.at[1], via4_last)
    landed = (rs.at[0], rs.at[1], rs_last)

    def sides(c):
        if c < 2:
            return (slice(0, ROWS), slice(0, 128)), (slice(0, ROWS), slice(128, 256))
        return (slice(0, 40), slice(0, 128)), (slice(40, PACKED), slice(0, 128))

    def z_send_to(c, i, src, dst, d):
        return send(src, dst, z_send.at[c, i], z_recv.at[c, i], at_z(d))

    def z_first(c):
        a, b = sides(c)
        at_b = (slice(0, PACKED - 40), slice(0, 128)) if c == 2 else (slice(0, ROWS), slice(0, 128))
        z_copies[c] = [
            z_send_to(c, 0, sums[c].at[(4,) + a], via_4[c].at[0], 2),
            z_send_to(c, 1, sums[c].at[(4,) + b], via_4[c].at[(1,) + at_b], 6),
            z_send_to(c, 2, sums[c].at[3], via_3[c].at[0], 1),
            z_send_to(c, 3, sums[c].at[5], via_3[c].at[1], 7),
        ]

    def z_direct(c):
        z_later[c] = [
            z_send_to(c, 4, sums[c].at[1], landed[c].at[0], 1),
            z_send_to(c, 5, sums[c].at[7], landed[c].at[1], 7),
        ]

    def relay(c):
        for copy in z_copies[c]:
            copy.wait_recv()
        a, b = sides(c)
        at_b = (slice(0, PACKED - 40), slice(0, 128)) if c == 2 else (slice(0, ROWS), slice(0, 128))
        store = sums[c]
        store[2] = store[2] + via_3[c][0]
        store[(2,) + a] = store[(2,) + a] + via_4[c][0]
        store[6] = store[6] + via_3[c][1]
        store[(6,) + b] = store[(6,) + b] + via_4[c][(1,) + at_b]
        z_later[c] += [
            z_send_to(c, 6, store.at[2], landed[c].at[2], 2),
            z_send_to(c, 7, store.at[6], landed[c].at[3], 6),
        ]

    def summed(c):
        for copy in z_later[c]:
            copy.wait_recv()
        got = landed[c]
        return sums[c][0] + ((got[0] + got[1]) + (got[2] + got[3]))

    def multiply(c):
        part[c] = product(c).reshape(NZ, ROWS, WIDE)
        z_first(c)

    def multiply_last():
        total = product(2)
        part_last[:, 0:ROWS, :] = total[:, 0:128].reshape(NZ, ROWS, 128)
        rest = jnp.concatenate(
            [total[:, 128:144], jnp.zeros((SET, 112), jnp.float32)], axis=1
        )
        for b in range(SET // 128):
            tile = jnp.transpose(rest[128 * b : 128 * b + 128])[0:REST]
            part_last[2 * b, ROWS:PACKED, 0:ROWS] = tile[:, 0:ROWS]
            part_last[2 * b + 1, ROWS:PACKED, 0:ROWS] = tile[:, ROWS : 2 * ROWS]
        z_first(2)

    def code(values, tile, rows):
        most = jnp.maximum(jnp.max(jnp.abs(values), axis=0, keepdims=True), TINY)
        scale[tile : tile + 1, :] = most * (1.0 / TOP)
        codes = jnp.round(values * (TOP / most)).astype(jnp.int32)
        if rows > values.shape[0]:
            codes = jnp.concatenate(
                [codes, jnp.zeros((rows - values.shape[0], 128), jnp.int32)], axis=0
            )
        return codes.astype(jnp.int16)

    turn = grp * (COLS % 128)

    def y_move(c, i, owner, cols, d):
        ref = fr.at[owner, :, cols]
        return send(ref, ref, y_send.at[c, i], y_recv.at[c, i], at_y(d))

    def back(d):
        return lax.rem(y + NY - d, NY)

    def y_relay(c):
        first = c * WIDE
        cols, left, right = pl.ds(first, WIDE), pl.ds(first, 128), pl.ds(first + 128, 128)
        later = []
        for i, (d, side, on) in enumerate(((2, left, 1), (6, right, 7))):
            y_copies[c][i].wait_recv()
            later.append(y_move(c, 4 + i, back(d), side, d))
            later.append(y_move(c, 6 + i, back(d), cols, on))
        y_copies[c] += later

    def update(c):
        first = c * WIDE
        total = summed(c)
        driver = drv_in[:, first : first + WIDE].astype(jnp.float32)
        total = (driver + total) / gap[:, first : first + WIDE]
        for j in range(2):
            tile = pltpu.roll(total[:, 128 * j : 128 * j + 128], turn, axis=1)
            lanes = slice(first + 128 * j, first + 128 * j + 128)
            fr[y, :, lanes] = code(tile, 2 * c + j, ROWS)
        cols = pl.ds(first, WIDE)
        y_copies[c] = [y_move(c, i, y, cols, d) for i, d in enumerate((2, 6, 1, 7))]
        cross(fr.at[y, :, cols], out.at[y, core, :, cols], c, 0)

    def cross(src, dst, kind, d):
        c_copies.append(send(src, dst, c_send.at[kind, d], c_recv.at[kind, d], sibling))

    def spread(c):
        cols = pl.ds(c * WIDE, WIDE)
        copies = y_copies[c]
        for waits, d in (((), 2), ((), 6), ((2,), 1), ((3,), 7), ((5,), 3), ((7,), 5), ((4, 6), 4)):
            for i in waits:
                copies[i].wait_recv()
            cross(fr.at[back(d), :, cols], out.at[back(d), core, :, cols], c, d)
        copy = pltpu.make_async_copy(fr.at[:, :, cols], out.at[:, core, :, cols], o_sem.at[c])
        copy.start()
        o_copies.append(copy)

    def update_last():
        total = (drv_last[...] + summed(2)) / gap_last[...]
        total = jnp.concatenate(
            [pltpu.roll(total[0:ROWS], turn, axis=1), total[ROWS:PACKED]], axis=0
        )
        fr_last[y] = code(total, 4, TILED)
        fr_scale[y] = scale[...]
        copies = []
        for d in FAR:
            for i, ref in enumerate((fr_scale.at[y], fr_last.at[y])):
                copies.append(
                    send(ref, ref, y_send.at[2 + i, d - 1], y_recv.at[2 + i, d - 1], at_y(d))
                )
        cross(fr_scale.at[y], out_scale.at[y, core], 2, 0)
        cross(fr_last.at[y], out_last.at[y, core], 3, 0)
        return copies

    def spread_last(copies):
        for i, d in enumerate(FAR):
            owner = lax.rem(y + NY - d, NY)
            copies[2 * i].wait_recv()
            cross(fr_scale.at[owner], out_scale.at[owner, core], 2, d)
            copies[2 * i + 1].wait_recv()
            cross(fr_last.at[owner], out_last.at[owner, core], 3, d)
        for kind, (src, dst) in enumerate(((fr_scale, out_scale), (fr_last, out_last))):
            copy = pltpu.make_async_copy(src, dst.at[:, core], o_sem.at[2 + kind])
            copy.start()
            o_copies.append(copy)

    scale[...] = jnp.zeros(scale.shape, jnp.float32)
    part_last[:, ROWS:PACKED, :] = jnp.zeros((NZ, REST, 128), jnp.float32)
    multiply(0)
    multiply(1)
    z_direct(0)
    relay(0)
    multiply_last()
    z_direct(1)
    relay(1)
    z_direct(2)
    update(0)
    relay(2)
    update(1)
    y_relay(0)
    last = update_last()
    y_relay(1)
    spread(0)
    spread(1)
    spread_last(last)
    for copy in c_copies:
        copy.wait_recv()
    for copy in o_copies:
        copy.wait()
    for copy in started:
        copy.wait_send()


def place_kernel(codes, last, scale, out, rest):
    tall = out.shape[0]
    rows = pl.ds(pl.multiple_of(pl.program_id(0) * tall, tall), tall)
    lane = lax.broadcasted_iota(jnp.int32, (tall, 128), 1)

    def value(coded):
        return coded.astype(jnp.int32).astype(jnp.float32)

    def tile(g, j):
        at = (g // 2, g % 2)
        coded = codes[at + (slice(None), slice(128 * j, 128 * j + 128))] if j < 4 else last[at + (rows,)]
        return value(coded) * scale[at + (slice(j, j + 1),)]

    @pl.when(pl.program_id(0) == 0)
    def _():
        lines = [
            value(last[g // 2, g % 2, ROWS:TILED, :])[0:REST] * scale[g // 2, g % 2, 4:5, :]
            for g in range(2 * NY)
        ]
        rest[...] = jnp.transpose(jnp.concatenate(lines, axis=0))

    mine = rest[rows, :]
    before = None
    for g in range(2 * NY):
        edge = REST * g
        for j in range(5):
            now = tile(g, j)
            first = 128 * (5 * g + j)
            out[:, first : first + 128] = now if before is None else jnp.where(lane < edge, before, now)
            before = now
        before = jnp.where(lane < edge, before, mine)
    out[:, VP - 128 : VP] = before


def shards(amplitudes, integrals, hole_ints, driver, e_occ, e_virt, occ_pairs, virt_pairs):
    dma = pltpu.SemaphoreType.DMA
    bf16, f32, i16 = jnp.bfloat16, jnp.float32, jnp.int16
    codes, last, scale = pl.pallas_call(
        ladder_kernel,
        out_shape=[
            jax.ShapeDtypeStruct((NY, 2, ROWS, LAST), i16),
            jax.ShapeDtypeStruct((NY, 2, TILED, 128), i16),
            jax.ShapeDtypeStruct((NY, 2, 8, 128), f32),
        ],
        in_specs=[pl.BlockSpec(memory_space=pl.ANY)] * 8,
        out_specs=[pl.BlockSpec(memory_space=pl.ANY)] * 3,
        scratch_shapes=[
            pltpu.VMEM((ROWS, VP), bf16),
            pltpu.VMEM((COLS, DEPTH), bf16),
            pltpu.VMEM((ROWS, COLS), bf16),
            pltpu.VMEM((ROWS, SET * NX), bf16),
            pltpu.VMEM((SET, NX * 128), bf16),
            pltpu.VMEM((1, 128), f32),
            pltpu.VMEM((288,), f32),
            pltpu.VMEM((2, ROWS), jnp.int32),
            pltpu.VMEM((2, COLS), jnp.int32),
            pltpu.VMEM((TALL, LANES), bf16),
            pltpu.VMEM((TALL, DEEP), bf16),
            pltpu.VMEM((NX * 128, FRAME), bf16),
            pltpu.VMEM((NZ, ROWS, DEEP), bf16),
            pltpu.VMEM((NZ, ROWS, DEEP), bf16),
            pltpu.VMEM((SET, NX * 128), bf16),
            pltpu.VMEM((2, NZ, ROWS, WIDE), f32),
            pltpu.VMEM((NZ, PACKED, 128), f32),
            pltpu.VMEM((2, 2, ROWS, WIDE), f32),
            pltpu.VMEM((2, PACKED, 128), f32),
            pltpu.VMEM((2, 2, ROWS, 128), f32),
            pltpu.VMEM((2, 40, 128), f32),
            pltpu.VMEM((2, 4, ROWS, WIDE), f32),
            pltpu.VMEM((4, PACKED, 128), f32),
            pltpu.VMEM((8, 128), f32),
            pltpu.VMEM((NY, ROWS, LAST), i16),
            pltpu.VMEM((NY, TILED, 128), i16),
            pltpu.VMEM((NY, 8, 128), f32),
            pltpu.VMEM((ROWS, COLS), f32),
            pltpu.VMEM((PACKED, 128), f32),
            pltpu.VMEM((PACKED, 128), f32),
            dma((12,)),
            dma((3, 4, 2)), dma((3, 4, 2)),
            dma((7,)), dma((7,)),
            dma((7,)), dma((7,)),
            dma((12,)), dma((12,)),
            dma((3, 8)), dma((3, 8)),
            dma((4, 8)), dma((4, 8)),
            dma((4, 8)), dma((4, 8)),
            dma((4,)),
        ],
        compiler_params=pltpu.CompilerParams(
            collective_id=0, has_side_effects=True, vmem_limit_bytes=62 * 2**20
        ),
        cost_estimate=pl.CostEstimate(
            flops=2 * SET * 4 * (DEPTH + ROWS) * COLS,
            bytes_accessed=8 * 2**20, transcendentals=0,
        ),
    )(
        amplitudes, integrals.T, hole_ints, driver, e_occ.reshape(1, 128),
        e_virt, occ_pairs, virt_pairs,
    )
    tall = 32
    return pl.pallas_call(
        place_kernel,
        grid=(ROWS // tall,),
        out_shape=jax.ShapeDtypeStruct((ROWS, VP), f32),
        in_specs=[
            pl.BlockSpec((NY, 2, tall, LAST), lambda i: (0, 0, i, 0)),
            pl.BlockSpec((NY, 2, TILED, 128), lambda i: (0, 0, 0, 0)),
            pl.BlockSpec((NY, 2, 8, 128), lambda i: (0, 0, 0, 0)),
        ],
        out_specs=pl.BlockSpec((tall, VP), lambda i: (i, 0)),
        scratch_shapes=[pltpu.VMEM((128, 128), f32)],
        compiler_params=pltpu.CompilerParams(vmem_limit_bytes=62 * 2**20),
    )(codes, last, scale)


def solution(mesh):
    placed = (
        P("pair", None),
        P("pair", "grp"),
        P(),
        P("pair", "grp"),
        P(),
        P(),
        P(None, "pair"),
        P(None, "grp"),
    )
    return jax.shard_map(
        shards, mesh=mesh, in_specs=placed, out_specs=P("pair", None), check_vma=False
    )
```

```python
import jax
import jax.numpy as jnp
from jax import lax
from jax.experimental import pallas as pl
from jax.experimental.pallas import tpu as pltpu
from jax.sharding import PartitionSpec as P

MESH = pl.DeviceIdType.MESH
NX, NY, NZ = 4, 8, 8
ROWS = 64
SET = NZ * ROWS
DEPTH = 324
COLS = 648
LANES = 384
FRAME = 768
SPARE = LANES - DEPTH
DEEP = NX * LANES
TALL = 656
VP = 10368
WIDE = 256
LAST = 2 * WIDE
REST = COLS - LAST - 128
PACKED = ROWS + REST
TILED = 80
TOP = 32767.0
TINY = 1e-33
FAR = (4, 3, 5, 2, 6, 1, 7)
NEAR = FAR[::-1]


def ladder_kernel(
    amp, ints, holes, drv, eocc, evirt, opairs, vpairs, out, out_last,
    amp_in, ints_in, drv_in, hole_own, hole_win, eocc_in, evirt_in, opairs_in, vpairs_in,
    own_vt, vt, ra, ap, al, hole_rel, part, part_last, via3, via3_last, via4, via4_last, rs, rs_last,
    scale, fr, fr_last, gap, gap_last, drv_last,
    in_sem, x_send, x_recv, a_send, a_recv, ay_send, ay_recv, ad_send, ad_recv,
    z_send, z_recv, y_send, y_recv, c_send, c_recv, o_sem,
):
    grp, pair = lax.axis_index("grp"), lax.axis_index("pair")
    y, core = grp // 2, lax.rem(grp, 2)
    x, z = pair // NZ, lax.rem(pair, NZ)

    def at_x(d):
        return (grp, lax.rem(x + d, NX) * NZ + z)

    def at_z(d):
        return (grp, x * NZ + lax.rem(z + d, NZ))

    def at_y(d):
        return (lax.rem(y + d, NY) * 2 + core, pair)

    sibling = (y * 2 + 1 - core, pair)

    loads = [
        pltpu.make_async_copy(ints, ints_in, in_sem.at[0]),
        pltpu.make_async_copy(amp, amp_in, in_sem.at[1]),
        pltpu.make_async_copy(
            holes.at[pl.ds(pl.multiple_of(pair * ROWS, ROWS), ROWS)], hole_own, in_sem.at[2]
        ),
        pltpu.make_async_copy(drv, drv_in, in_sem.at[11]),
        pltpu.make_async_copy(eocc, eocc_in, in_sem.at[3]),
        pltpu.make_async_copy(evirt, evirt_in, in_sem.at[4]),
        pltpu.make_async_copy(opairs, opairs_in, in_sem.at[5]),
        pltpu.make_async_copy(vpairs, vpairs_in, in_sem.at[6]),
    ]
    for k in range(NX):
        rows = pl.ds(pl.multiple_of(x * SET, SET), SET)
        cols = pl.ds(pl.multiple_of((k * NZ + z) // 2 * 128, 128), 128)
        loads.append(
            pltpu.make_async_copy(
                holes.at[rows, cols], hole_win.at[:, pl.ds(128 * k, 128)], in_sem.at[7 + k]
            )
        )
    for load in loads[:3]:
        load.start()

    barrier = pltpu.get_barrier_semaphore()
    peers = [at_x(d) for d in (1, 2, 3)] + [at_z(d) for d in FAR]
    peers += [at_y(d) for d in FAR] + [sibling]
    for peer in peers:
        pl.semaphore_signal(barrier, inc=1, device_id=peer, device_id_type=MESH)
    for load in loads[3:]:
        load.start()

    half = lax.rem(z, 2) * ROWS + ROWS - 16
    started = []

    def settle(count):
        for copy in started[:count]:
            copy.wait_send()
        del started[:count]

    def send(src, dst, send_sem, recv_sem, device):
        copy = pltpu.make_async_remote_copy(
            src_ref=src, dst_ref=dst, send_sem=send_sem, recv_sem=recv_sem,
            device_id=device, device_id_type=MESH,
        )
        copy.start()
        started.append(copy)
        return copy

    loads[0].wait()
    own_vt[COLS:TALL, :] = jnp.zeros((TALL - COLS, LANES), jnp.bfloat16)
    own_vt[0:COLS, 256:LANES] = jnp.zeros((COLS, LANES - 256), jnp.bfloat16)
    own_vt[0:COLS, 0:DEPTH] = ints_in[...]

    loads[1].wait()
    start = pl.multiple_of(grp * (COLS // 128) * 128, 128)
    window = amp_in[:, pl.ds(start, FRAME)].astype(jnp.float32)
    window = pltpu.roll(window, lax.rem(FRAME - grp * (COLS % 128), FRAME), axis=1)
    row = lax.broadcasted_iota(jnp.int32, (16, FRAME), 0)
    tail = jnp.where(row < SPARE - (ROWS - 16), 0.0, window[ROWS - 16 : ROWS])
    other = ROWS * (1 - lax.rem(z, 2)) + ROWS - 16
    for k in range(NX):
        for b in range(2):
            at = 128 * k + ROWS * b
            ra[at : at + ROWS - 16, :] = jnp.zeros((ROWS - 16, FRAME), jnp.bfloat16)
        ra[pl.ds(pl.multiple_of(128 * k + other, 16), 16), :] = jnp.zeros((16, FRAME), jnp.bfloat16)
    ra[pl.ds(pl.multiple_of(128 * x + half, 16), 16), :] = tail.astype(jnp.bfloat16)
    lane = lax.broadcasted_iota(jnp.int32, (128, 128), 1)
    for b in range(FRAME // 128):
        tall = min(128, TALL - 128 * b)
        block = jnp.concatenate(
            [window[:, 128 * b : 128 * b + 128], jnp.zeros((128 - ROWS, 128), jnp.float32)], axis=0
        )
        block = pltpu.roll(jnp.transpose(block), DEPTH - 256, axis=1)[0:tall]
        lines = slice(128 * b, 128 * b + tall)
        mixed = jnp.where(
            lane[0:tall] < DEPTH - 256, own_vt[lines, 256:LANES].astype(jnp.float32), block
        )
        own_vt[lines, 256:LANES] = mixed.astype(jnp.bfloat16)

    loads[2].wait()
    for k in range(NX):
        for t in range(NZ):
            owner = k * NZ + t
            at = k * LANES
            ap[t, :, at : at + DEPTH] = amp_in[:, owner * DEPTH : (owner + 1) * DEPTH]
            ap[t, :, at + DEPTH : at + LANES] = hole_own[:, owner * ROWS : owner * ROWS + SPARE]

    pl.semaphore_wait(barrier, len(peers))

    both = pl.ds(pl.multiple_of(core * 2 * LANES, 128), 2 * LANES)

    def unit_of(chip):
        rows = pl.ds(pl.multiple_of(lax.rem(chip, 2) * 32 + core * 16, 16), 16)
        return rows, pl.ds(pl.multiple_of(chip // 2 * LANES, 128), LANES)

    rows, lanes = unit_of(y)
    far_copies = [
        send(ap.at[lax.rem(z + d, NZ), rows, lanes], al.at[NZ - d, rows, lanes],
             a_send.at[d - 1], a_recv.at[d - 1], at_z(d))
        for d in (4, 3, 5)
    ]

    def x_sends(c, owner, d, slot, side=None):
        first, tall, wide = c * WIDE, (TALL - LAST if c == 2 else WIDE), WIDE
        if side is not None:
            first, tall, wide = first + 128 * side, 128, 128
        to = vt.at[pl.ds(first, tall), pl.ds(pl.multiple_of(owner * LANES, 128), LANES)]
        cells = ra.at[pl.ds(pl.multiple_of(128 * owner + half, 16), 16), pl.ds(first, wide)]
        return [
            send(own_vt.at[pl.ds(first, tall)] if owner is x else to, to,
                 x_send.at[c, slot, 0], x_recv.at[c, slot, 0], at_x(d)),
            send(cells, cells, x_send.at[c, slot, 1], x_recv.at[c, slot, 1], at_x(d)),
        ]

    x_copies = [[], [], []]

    def x_first(c):
        x_copies[c] = [x_sends(c, x, 1, 0), x_sends(c, x, 3, 1)]

    def x_second(c):
        for copies in x_copies[c]:
            for copy in copies:
                copy.wait_recv()
        x_copies[c] = [
            x_sends(c, lax.rem(x + 3, NX), 1, 2, 0),
            x_sends(c, lax.rem(x + 1, NX), 3, 3, 1),
        ]

    x_first(0)
    near_copies = [
        send(ap.at[lax.rem(z + d, NZ), :, both], al.at[NZ - d, :, both],
             a_send.at[d - 1], a_recv.at[d - 1], at_z(d))
        for d in (2, 6, 1, 7)
    ]
    x_first(1)

    vt[:, pl.ds(pl.multiple_of(x * LANES, 128), LANES)] = own_vt[...]
    al[0] = ap[z]

    for load in loads[3:]:
        load.wait()
    orbital = lax.broadcasted_iota(jnp.int32, (128, 128), 0)
    diagonal = orbital == lax.broadcasted_iota(jnp.int32, (128, 128), 1)

    def column(row):
        spread = jnp.where(diagonal, jnp.broadcast_to(row, (128, 128)), 0.0)
        return jnp.sum(spread, axis=1, keepdims=True)

    occ = column(eocc_in[...])
    hole_row = jnp.zeros((1, ROWS), jnp.float32)
    for s in range(2):
        labels = jnp.broadcast_to(opairs_in[s : s + 1, :], (128, ROWS))
        table = lax.broadcasted_iota(jnp.int32, (128, ROWS), 0)
        picked = jnp.where(labels == table, jnp.broadcast_to(occ, (128, ROWS)), 0.0)
        hole_row = hole_row + jnp.sum(picked, axis=0, keepdims=True)
    square = lax.broadcasted_iota(jnp.int32, (ROWS, ROWS), 0)
    square = square == lax.broadcasted_iota(jnp.int32, (ROWS, ROWS), 1)
    hole_col = jnp.sum(
        jnp.where(square, jnp.broadcast_to(hole_row, (ROWS, ROWS)), 0.0),
        axis=1, keepdims=True,
    )
    padded = jnp.concatenate([evirt_in[...].reshape(1, 288), jnp.zeros((1, 96), jnp.float32)], axis=1)
    virts = [column(padded[:, 128 * b : 128 * b + 128]) for b in range(3)]
    pair_row = jnp.zeros((1, COLS), jnp.float32)
    for s in range(2):
        labels = jnp.broadcast_to(vpairs_in[s : s + 1, :], (128, COLS))
        table = lax.broadcasted_iota(jnp.int32, (128, COLS), 0)
        picked = jnp.zeros((128, COLS), jnp.float32)
        for b in range(3):
            virt = jnp.broadcast_to(virts[b], (128, COLS))
            picked = jnp.where(labels == table + 128 * b, virt, picked)
        pair_row = pair_row + jnp.sum(picked, axis=0, keepdims=True)
    gap[...] = pair_row - hole_col

    def turned(block):
        tile = jnp.concatenate([block, jnp.zeros((ROWS, 128 - REST), jnp.float32)], axis=1)
        tile = jnp.concatenate([tile, jnp.zeros((128 - ROWS, 128), jnp.float32)], axis=0)
        return jnp.transpose(tile)[0:REST, 0:ROWS]

    gap_last[...] = jnp.ones(gap_last.shape, jnp.float32)
    gap_last[0:ROWS, :] = gap[:, LAST : LAST + 128]
    gap_last[ROWS:PACKED, 0:ROWS] = turned(gap[:, COLS - REST : COLS])
    drv_last[...] = jnp.zeros(drv_last.shape, jnp.float32)
    drv_last[0:ROWS, :] = drv_in[:, LAST : LAST + 128].astype(jnp.float32)
    drv_last[ROWS:PACKED, 0:ROWS] = turned(drv_in[:, COLS - REST : COLS].astype(jnp.float32))

    for r in range(NZ):
        lines = pl.ds(pl.multiple_of(lax.rem(z + r, NZ) * ROWS, ROWS), ROWS)
        hole_rel[r * ROWS : (r + 1) * ROWS, :] = hole_win[lines, :]

    ad_copies = []

    def share(ref, slot):
        ad_copies.append(send(ref, ref, ad_send.at[slot], ad_recv.at[slot], sibling))

    far = pl.ds(3, 3)
    for copy in far_copies:
        copy.wait_recv()
    own = al.at[far, rows, lanes]
    ay_copies = [
        send(own, own, ay_send.at[d - 1], ay_recv.at[d - 1], at_y(d)) for d in FAR
    ]
    share(own, 0)
    x_second(0)
    for slot, d in ((2, 1), (3, 7), (0, 2), (1, 6)):
        near_copies[slot].wait_recv()
        share(al.at[NZ - d, :, both], 8 + slot)
    x_second(1)
    before = len(started)
    x_copies[2] = [x_sends(2, x, d, d - 1) for d in (2, 1, 3)]
    for d in NEAR:
        ay_copies[FAR.index(d)].wait_recv()
        rows, lanes = unit_of(lax.rem(y + NY - d, NY))
        share(al.at[far, rows, lanes], d)
    for copy in ad_copies:
        copy.wait_recv()

    def product(c):
        first, tall = c * WIDE, (TALL - LAST if c == 2 else WIDE)
        for copies in x_copies[c]:
            for copy in copies:
                copy.wait_recv()
        return lax.dot_general(
            al[...].reshape(SET, DEEP), vt[first : first + tall, :],
            (((1,), (1,)), ((), ())), preferred_element_type=jnp.float32,
        ) + jnp.dot(
            hole_rel[...], ra[:, first : first + tall], preferred_element_type=jnp.float32
        )

    z_copies, z_later, y_copies = [None] * 3, [None] * 3, [None] * 3
    c_copies, o_copies = [], []

    sums = (part.at[0], part.at[1], part_last)
    via_3 = (via3.at[0], via3.at[1], via3_last)
    via_4 = (via4.at[0], via4.at[1], via4_last)
    landed = (rs.at[0], rs.at[1], rs_last)

    def sides(c):
        if c < 2:
            return (slice(0, ROWS), slice(0, 128)), (slice(0, ROWS), slice(128, 256))
        return (slice(0, 40), slice(0, 128)), (slice(40, PACKED), slice(0, 128))

    def z_send_to(c, i, src, dst, d):
        return send(src, dst, z_send.at[c, i], z_recv.at[c, i], at_z(d))

    def z_first(c):
        a, b = sides(c)
        at_b = (slice(0, PACKED - 40), slice(0, 128)) if c == 2 else (slice(0, ROWS), slice(0, 128))
        z_copies[c] = [
            z_send_to(c, 0, sums[c].at[(4,) + a], via_4[c].at[0], 2),
            z_send_to(c, 1, sums[c].at[(4,) + b], via_4[c].at[(1,) + at_b], 6),
            z_send_to(c, 2, sums[c].at[3], via_3[c].at[0], 1),
            z_send_to(c, 3, sums[c].at[5], via_3[c].at[1], 7),
        ]

    def z_direct(c):
        z_later[c] = [
            z_send_to(c, 4, sums[c].at[1], landed[c].at[0], 1),
            z_send_to(c, 5, sums[c].at[7], landed[c].at[1], 7),
        ]

    def relay(c):
        for copy in z_copies[c]:
            copy.wait_recv()
        a, b = sides(c)
        at_b = (slice(0, PACKED - 40), slice(0, 128)) if c == 2 else (slice(0, ROWS), slice(0, 128))
        store = sums[c]
        store[2] = store[2] + via_3[c][0]
        store[(2,) + a] = store[(2,) + a] + via_4[c][0]
        store[6] = store[6] + via_3[c][1]
        store[(6,) + b] = store[(6,) + b] + via_4[c][(1,) + at_b]
        z_later[c] += [
            z_send_to(c, 6, store.at[2], landed[c].at[2], 2),
            z_send_to(c, 7, store.at[6], landed[c].at[3], 6),
        ]

    def summed(c):
        for copy in z_later[c]:
            copy.wait_recv()
        got = landed[c]
        return sums[c][0] + ((got[0] + got[1]) + (got[2] + got[3]))

    def multiply(c):
        part[c] = product(c).reshape(NZ, ROWS, WIDE)
        z_first(c)

    def multiply_last():
        total = product(2)
        part_last[:, 0:ROWS, :] = total[:, 0:128].reshape(NZ, ROWS, 128)
        rest = jnp.concatenate(
            [total[:, 128:144], jnp.zeros((SET, 112), jnp.float32)], axis=1
        )
        for b in range(SET // 128):
            tile = jnp.transpose(rest[128 * b : 128 * b + 128])[0:REST]
            part_last[2 * b, ROWS:PACKED, 0:ROWS] = tile[:, 0:ROWS]
            part_last[2 * b + 1, ROWS:PACKED, 0:ROWS] = tile[:, ROWS : 2 * ROWS]
        z_first(2)

    def code(values, tile):
        most = jnp.maximum(jnp.max(jnp.abs(values), axis=0, keepdims=True), TINY)
        power = jnp.ceil(jnp.log2(most) + 1e-3)
        scale[tile : tile + 1, :] = power
        return jnp.round(values * (TOP * jnp.exp2(-power))).astype(jnp.int32)

    turn = grp * (COLS % 128)

    def y_move(c, i, owner, cols, d):
        ref = fr.at[owner, :, cols]
        return send(ref, ref, y_send.at[c, i], y_recv.at[c, i], at_y(d))

    def back(d):
        return lax.rem(y + NY - d, NY)

    def y_relay(c):
        first = c * WIDE
        cols, left, right = pl.ds(first, WIDE), pl.ds(first, 128), pl.ds(first + 128, 128)
        later = []
        for i, (d, side, on) in enumerate(((2, left, 1), (6, right, 7))):
            y_copies[c][i].wait_recv()
            later.append(y_move(c, 4 + i, back(d), side, d))
            later.append(y_move(c, 6 + i, back(d), cols, on))
        y_copies[c] += later

    def update(c):
        first = c * WIDE
        total = summed(c)
        driver = drv_in[:, first : first + WIDE].astype(jnp.float32)
        total = (driver + total) / gap[:, first : first + WIDE]
        for j in range(2):
            tile = pltpu.roll(total[:, 128 * j : 128 * j + 128], turn, axis=1)
            lanes = slice(first + 128 * j, first + 128 * j + 128)
            fr[y, :, lanes] = code(tile, 2 * c + j).astype(jnp.int16)
        cols = pl.ds(first, WIDE)
        y_copies[c] = [y_move(c, i, y, cols, d) for i, d in enumerate((2, 6, 1, 7))]
        cross(fr.at[y, :, cols], out.at[y, core, :, cols], c, 0)

    def cross(src, dst, kind, d):
        c_copies.append(send(src, dst, c_send.at[kind, d], c_recv.at[kind, d], sibling))

    def spread(c):
        cols = pl.ds(c * WIDE, WIDE)
        copies = y_copies[c]
        for waits, d in (((), 2), ((), 6), ((2,), 1), ((3,), 7), ((5,), 3), ((7,), 5), ((4, 6), 4)):
            for i in waits:
                copies[i].wait_recv()
            cross(fr.at[back(d), :, cols], out.at[back(d), core, :, cols], c, d)
        copy = pltpu.make_async_copy(fr.at[:, :, cols], out.at[:, core, :, cols], o_sem.at[c])
        copy.start()
        o_copies.append(copy)

    def update_last():
        total = (drv_last[...] + summed(2)) / gap_last[...]
        total = jnp.concatenate(
            [pltpu.roll(total[0:ROWS], turn, axis=1), total[ROWS:PACKED]], axis=0
        )
        codes = code(total, 4)
        powers = scale[...].astype(jnp.int32)
        fr_last[y] = jnp.concatenate([codes, powers], axis=0).astype(jnp.int16)
        ref = fr_last.at[y]
        copies = [
            send(ref, ref, y_send.at[2, d - 1], y_recv.at[2, d - 1], at_y(d)) for d in FAR
        ]
        cross(ref, out_last.at[y, core], 2, 0)
        return copies

    def spread_last(copies):
        for d in NEAR:
            copies[FAR.index(d)].wait_recv()
            cross(fr_last.at[back(d)], out_last.at[back(d), core], 2, d)
        copy = pltpu.make_async_copy(fr_last, out_last.at[:, core], o_sem.at[2])
        copy.start()
        o_copies.append(copy)

    scale[...] = jnp.zeros(scale.shape, jnp.float32)
    part_last[:, ROWS:PACKED, :] = jnp.zeros((NZ, REST, 128), jnp.float32)
    multiply(0)
    multiply(1)
    z_direct(0)
    settle(before)
    relay(0)
    multiply_last()
    z_direct(1)
    relay(1)
    z_direct(2)
    update(0)
    relay(2)
    before = len(started)
    update(1)
    y_relay(0)
    last = update_last()
    settle(before)
    y_relay(1)
    spread(0)
    spread(1)
    spread_last(last)
    for copy in c_copies:
        copy.wait_recv()
    for copy in o_copies:
        copy.wait()
    for copy in started:
        copy.wait_send()


def place_kernel(codes, last, out, rest):
    tall = out.shape[0]
    rows = pl.ds(pl.multiple_of(pl.program_id(0) * tall, tall), tall)
    lane = lax.broadcasted_iota(jnp.int32, (tall, 128), 1)

    def value(coded):
        return coded.astype(jnp.int32).astype(jnp.float32)

    ends = [value(last[g // 2, g % 2, ROWS:TILED, :]) for g in range(2 * NY)]
    scale = [jnp.exp2(end[REST : 2 * REST]) * (1.0 / TOP) for end in ends]

    def tile(g, j):
        at = (g // 2, g % 2)
        coded = codes[at + (slice(None), slice(128 * j, 128 * j + 128))] if j < 4 else last[at + (rows,)]
        return value(coded) * scale[g][j : j + 1]

    @pl.when(pl.program_id(0) == 0)
    def _():
        lines = [ends[g][0:REST] * scale[g][4:5] for g in range(2 * NY)]
        rest[...] = jnp.transpose(jnp.concatenate(lines, axis=0))

    mine = rest[rows, :]
    before = None
    for g in range(2 * NY):
        edge = REST * g
        for j in range(5):
            now = tile(g, j)
            first = 128 * (5 * g + j)
            out[:, first : first + 128] = now if before is None else jnp.where(lane < edge, before, now)
            before = now
        before = jnp.where(lane < edge, before, mine)
    out[:, VP - 128 : VP] = before


def shards(amplitudes, integrals, hole_ints, driver, e_occ, e_virt, occ_pairs, virt_pairs):
    dma = pltpu.SemaphoreType.DMA
    bf16, f32, i16 = jnp.bfloat16, jnp.float32, jnp.int16
    codes, last = pl.pallas_call(
        ladder_kernel,
        out_shape=[
            jax.ShapeDtypeStruct((NY, 2, ROWS, LAST), i16),
            jax.ShapeDtypeStruct((NY, 2, TILED, 128), i16),
        ],
        in_specs=[pl.BlockSpec(memory_space=pl.ANY)] * 8,
        out_specs=[pl.BlockSpec(memory_space=pl.ANY)] * 2,
        scratch_shapes=[
            pltpu.VMEM((ROWS, VP), bf16),
            pltpu.VMEM((COLS, DEPTH), bf16),
            pltpu.VMEM((ROWS, COLS), bf16),
            pltpu.VMEM((ROWS, SET * NX), bf16),
            pltpu.VMEM((SET, NX * 128), bf16),
            pltpu.VMEM((1, 128), f32),
            pltpu.VMEM((288,), f32),
            pltpu.VMEM((2, ROWS), jnp.int32),
            pltpu.VMEM((2, COLS), jnp.int32),
            pltpu.VMEM((TALL, LANES), bf16),
            pltpu.VMEM((TALL, DEEP), bf16),
            pltpu.VMEM((NX * 128, FRAME), bf16),
            pltpu.VMEM((NZ, ROWS, DEEP), bf16),
            pltpu.VMEM((NZ, ROWS, DEEP), bf16),
            pltpu.VMEM((SET, NX * 128), bf16),
            pltpu.VMEM((2, NZ, ROWS, WIDE), f32),
            pltpu.VMEM((NZ, PACKED, 128), f32),
            pltpu.VMEM((2, 2, ROWS, WIDE), f32),
            pltpu.VMEM((2, PACKED, 128), f32),
            pltpu.VMEM((2, 2, ROWS, 128), f32),
            pltpu.VMEM((2, 40, 128), f32),
            pltpu.VMEM((2, 4, ROWS, WIDE), f32),
            pltpu.VMEM((4, PACKED, 128), f32),
            pltpu.VMEM((8, 128), f32),
            pltpu.VMEM((NY, ROWS, LAST), i16),
            pltpu.VMEM((NY, TILED, 128), i16),
            pltpu.VMEM((ROWS, COLS), f32),
            pltpu.VMEM((PACKED, 128), f32),
            pltpu.VMEM((PACKED, 128), f32),
            dma((12,)),
            dma((3, 4, 2)), dma((3, 4, 2)),
            dma((7,)), dma((7,)),
            dma((7,)), dma((7,)),
            dma((12,)), dma((12,)),
            dma((3, 8)), dma((3, 8)),
            dma((3, 8)), dma((3, 8)),
            dma((3, 8)), dma((3, 8)),
            dma((3,)),
        ],
        compiler_params=pltpu.CompilerParams(
            collective_id=0, has_side_effects=True, vmem_limit_bytes=62 * 2**20
        ),
        cost_estimate=pl.CostEstimate(
            flops=2 * SET * 4 * (DEPTH + ROWS) * COLS,
            bytes_accessed=8 * 2**20, transcendentals=0,
        ),
    )(
        amplitudes, integrals.T, hole_ints, driver, e_occ.reshape(1, 128),
        e_virt, occ_pairs, virt_pairs,
    )
    tall = 32
    return pl.pallas_call(
        place_kernel,
        grid=(ROWS // tall,),
        out_shape=jax.ShapeDtypeStruct((ROWS, VP), f32),
        in_specs=[
            pl.BlockSpec((NY, 2, tall, LAST), lambda i: (0, 0, i, 0)),
            pl.BlockSpec((NY, 2, TILED, 128), lambda i: (0, 0, 0, 0)),
        ],
        out_specs=pl.BlockSpec((tall, VP), lambda i: (i, 0)),
        scratch_shapes=[pltpu.VMEM((128, 128), f32)],
        compiler_params=pltpu.CompilerParams(vmem_limit_bytes=62 * 2**20),
    )(codes, last)


def solution(mesh):
    placed = (
        P("pair", None),
        P("pair", "grp"),
        P(),
        P("pair", "grp"),
        P(),
        P(),
        P(None, "pair"),
        P(None, "grp"),
    )
    return jax.shard_map(
        shards, mesh=mesh, in_specs=placed, out_specs=P("pair", None), check_vma=False
    )
```
